128 devices in a mesh: replica: 16 (over y, z_hi, core), expert: 8 (over x, z_lo).
Axes of the slice: x: 4, y: 4, z: 4 (z_hi: 2, z_lo: 2; z = z_hi * 2 + z_lo), core: 2. Of those that a mesh axis runs over, the one named last changes fastest.
Arguments:
- tokens: bfloat16 [16384, 2048], P(('replica', 'expert')), may hold values from -6 to 6
- route_ids: int32 [16384, 1], P(('replica', 'expert')), may hold values from 0 to 7; in each aligned block of 128 rows (0 to 127, 128 to 255, ...) at most 24 rows name the same one
- route_logits: float32 [16384, 8], P(('replica', 'expert')), may hold values from -12 to 320, as said below
- grad_out: bfloat16 [16384, 2048], P(('replica', 'expert')), may hold values from -6 to 6
- w_gate: bfloat16 [16, 8, 2048, 768], P('replica', 'expert'), may hold values from -0.125 to 0.125
- w_up: bfloat16 [16, 8, 2048, 768], P('replica', 'expert'), may hold values from -0.125 to 0.125
- w_down: bfloat16 [16, 8, 768, 2048], P('replica', 'expert'), may hold values from -0.21875 to 0.21875
- drift: float32 [16, 2, 2048, 1024], P('replica', None, None, 'expert'), may hold values from -6 to 6
- outer: float32 [2, 2048, 1024], P(None, 'replica', 'expert'), may hold values from -6 to 6
- momentum: float32 [2, 2048, 1024], P(None, 'replica', 'expert'), may hold values from -4 to 4
- inner_now: bfloat16 [16, 2, 2048, 1024], P('replica', None, None, 'expert'), may hold values from -6 to 6
Outputs:
- grad_tokens: bfloat16 [16384, 2048], P(('replica', 'expert'))
- grad_logits: float32 [16384, 8], P(('replica', 'expert'))
- grad_gate: bfloat16 [16, 8, 2048, 768], P('replica', 'expert')
- grad_up: bfloat16 [16, 8, 2048, 768], P('replica', 'expert')
- grad_down: bfloat16 [16, 8, 768, 2048], P('replica', 'expert')
- new_outer: float32 [2, 2048, 1024], P(None, 'replica', 'expert')
- new_momentum: float32 [2, 2048, 1024], P(None, 'replica', 'expert')
- merged: bfloat16 [16, 2, 2048, 1024], P('replica', None, None, 'expert')
The draws below stay inside these ranges and needn't reach their ends.
Inputs may be any that keep to these rules, and one draw needn't show every extreme that they name: `route_ids`: each token names one expert of its replica's group; the rows of one device name no expert more than 24 times, and in every draw the rows of some device name some expert exactly 24 times. `route_logits`: the first 1 column are the logits of the experts named in route_ids.
All inputs are finite; a program needn't handle non-finite values.
Results may differ from the reference program's by a relative error of at most 0.014.
Values may be sent and summed in bfloat16 or wider, within the bound.
A program may use at most 128 MiB of HBM per device.

```python
import math
import jax
import jax.numpy as jnp
import numpy as np
from jax import lax

D = 2048
FF = 768
KV = 1024
TOP = 8
TOP_WIN = 1
FLAYERS = 2
TOK_DEV = 128
EXPERTS = 8
CAP = 24
TOKENS = 16384
N_REPLICA = 16
N_EXPERT = 8


def draw_route_logits(key, part):
    key = jax.random.fold_in(key, 7)
    base_key = jax.random.fold_in(key, 0)
    return jnp.clip(2.0 * jax.random.normal(base_key, (TOKENS, TOP), jnp.float32), -12.0, 12.0)


def spiked(result, own_key, source, target, shards_of, factor):
    owner, partner = [(jnp.arange(result.shape[axis_at]) // (result.shape[axis_at] // shards_of)).reshape([-1 if axis == axis_at else 1 for axis in range(result.ndim)]) for axis_at in (source, target)]
    chosen = jax.random.permutation(own_key, shards_of)[partner]
    strong = (owner == chosen) | (owner == (partner + shards_of // 2) % shards_of)
    return jnp.where(strong, factor * result, result)


def levels(rng, dims, cuts, least, top_value):
    level, own = 1.0, jax.random.fold_in(rng, 6)
    for position, shards_of in cuts:
        steps = jnp.exp(jax.random.uniform(jax.random.fold_in(own, position), (shards_of,), jnp.float32, least / len(cuts), top_value / len(cuts)))
        level = level * jnp.repeat(steps, dims[position] // shards_of).reshape([-1 if axis == position else 1 for axis in range(len(dims))])
    return level


def deal_out(own_key, own, number, rows, amount, top, limit, skew):
    sequence = jax.random.permutation(own_key, amount)
    crowded, usual = shares(amount, rows * top, limit, skew, True), shares(amount, rows * top, limit, skew, False)
    places = jnp.arange(amount)

    def named(sizes, turn):
        used = int((sizes > 0).sum())
        fixed = max(1, used // 4)
        shifted = fixed + (places - fixed + turn * (used - fixed)) % max(1, amount - fixed)
        return jnp.zeros((amount,), jnp.int32).at[sequence[jnp.where(places < fixed, places, shifted)]].set(jnp.asarray(sizes, jnp.int32))

    sizes = jnp.where(number % 4 == 0, named(crowded, number // 4), named(usual, number - number // 4 - 1))
    mixed = jax.random.permutation(jax.random.fold_in(own, 3), amount)
    giver, taker = mixed[0:amount // 2 * 2:2], mixed[1:amount // 2 * 2:2]
    slack = jnp.minimum(sizes[giver] - 1, limit - sizes[taker]) // 2
    slack = jnp.where((giver == sequence[0]) | (taker == sequence[0]) | (sizes[taker] == 0), 0, jnp.maximum(slack, 0))
    shifted = jax.random.randint(jax.random.fold_in(own, 4), (amount // 2,), 0, 1 << 20) % (slack + 1)
    sizes = sizes.at[giver].add(-shifted).at[taker].add(shifted)
    labels = jnp.searchsorted(jnp.cumsum(sizes), jnp.arange(rows * top), side="right").astype(jnp.int32)
    listing = labels.reshape(top, rows).T
    listing = listing[jax.random.permutation(jax.random.fold_in(own, 1), rows)]
    turn = jax.random.randint(jax.random.fold_in(own, 2), (rows, 1), 0, top)
    return jnp.take_along_axis(listing, (jnp.arange(top)[None, :] + turn) % top, axis=1)


def shares(number_of, total, bound, slope, full):
    weights = [(1 << 20) // math.isqrt(grade ** slope) + 1 for grade in range(1, number_of + 1)]
    largest = bound if full else min(bound, max(-(-total // number_of), total * weights[0] // sum(weights)))
    least = 1 if total - largest >= number_of - 1 else 0
    counts, surplus = [largest] + [least] * (number_of - 1), total - largest - least * (number_of - 1)
    while surplus > 0:
        candidates = [i for i in range(1, number_of) if counts[i] < largest] or [i for i in range(1, number_of) if counts[i] < bound]
        pool, left = sum([weights[i] for i in candidates]), surplus
        for i in candidates:
            more = min(bound - counts[i], max(1, left * weights[i] // pool), surplus)
            counts[i] = counts[i] + more
            surplus = surplus - more
    return np.array(counts)


def noise(own_key, extent, deviation, reach, cuts=(), held_as=jnp.bfloat16):
    result = jax.random.normal(own_key, extent, jnp.float32) * deviation
    if len(cuts) > 0:
        result = levels(own_key, extent, cuts, -0.22, 0.18) * result
    return jnp.clip(result, min=-reach, max=reach).astype(held_as)


def heavy_noise(key, shape, scale, bound, cuts, heavy, held_as=jnp.bfloat16):
    entries = scale * jax.random.normal(key, shape, jnp.float32)
    if cuts:
        entries = entries * levels(key, shape, cuts, -0.22, 0.18)
    return jnp.clip(spiked(entries, jax.random.fold_in(key, 3), *heavy), -bound, bound).astype(held_as)


def setup_inputs(seed: int = 0) -> dict:
    key_list = jax.random.split(jax.random.key(seed), 12)
    tokens = noise(key_list[0], (TOKENS, D), 1.0, 6.0, ((0, 128),))
    route_ids_keys = jax.random.split(jax.random.fold_in(key_list[1], 1), TOKENS // TOK_DEV)
    route_ids_turns = jax.random.permutation(jax.random.fold_in(key_list[1], 3), TOKENS // TOK_DEV)
    route_ids = jax.vmap(lambda own, number: deal_out(jax.random.fold_in(key_list[1], 2), own, number, TOK_DEV, EXPERTS, TOP_WIN, CAP, 2))(route_ids_keys, route_ids_turns).reshape((TOKENS, TOP_WIN))
    route_logits = draw_route_logits(jax.random.fold_in(key_list[11], 71), 0)
    grad_out = noise(key_list[3], (TOKENS, D), 1.0, 6.0, ((0, 128),))
    w_gate = noise(key_list[4], (N_REPLICA, EXPERTS, D, FF), D ** -0.5, 0.125, ((0, 16), (1, 8)))
    w_up = noise(key_list[5], (N_REPLICA, EXPERTS, D, FF), D ** -0.5, 0.125, ((0, 16), (1, 8)))
    w_down = noise(key_list[6], (N_REPLICA, EXPERTS, FF, D), FF ** -0.5, 0.21875, ((0, 16), (1, 8)))
    drift = heavy_noise(key_list[7], (N_REPLICA, FLAYERS, D, KV), 1.0, 6.0, ((0, 16), (3, 8)), (0, 2, 16, 2.0), jnp.float32)
    outer = noise(key_list[8], (FLAYERS, D, KV), 1.0, 6.0, ((1, 16), (2, 8)), jnp.float32)
    momentum = noise(key_list[9], (FLAYERS, D, KV), 0.5, 4.0, ((1, 16), (2, 8)), jnp.float32)
    inner_now = noise(key_list[10], (N_REPLICA, FLAYERS, D, KV), 1.0, 6.0, ((0, 16), (3, 8)))
    return dict(tokens=tokens, route_ids=route_ids, route_logits=route_logits, grad_out=grad_out, w_gate=w_gate, w_up=w_up, w_down=w_down, drift=drift, outer=outer, momentum=momentum, inner_now=inner_now)


momentum_rate = 0.9
outer_rate = 0.7
mix_rate = 0.5


def replica_pass(operands):
    tokens, route_ids, route_logits, grad_out, w_gate, w_up, w_down = operands
    row_count = tokens.shape[0]
    pair_count = row_count * TOP_WIN
    chosen = CAP * N_EXPERT
    flat_ids = route_ids.reshape(pair_count)
    pair_tokens = jnp.repeat(tokens, TOP_WIN, axis=0)
    pair_grads = jnp.repeat(grad_out, TOP_WIN, axis=0)
    probability = jax.nn.softmax(route_logits, axis=-1)
    zero_half = jnp.zeros((), jnp.bfloat16)
    expert_list = jnp.arange(EXPERTS, dtype=jnp.int32)

    def select_rows(expert):
        picked = jnp.argsort((flat_ids != expert).astype(jnp.int32), stable=True)[:chosen]
        live_rows = (flat_ids[picked] == expert)[:, None]
        return picked, live_rows

    def forward_one(accumulated, operand):
        gate_weight, up_weight, down_weight, expert = operand
        picked, live_rows = select_rows(expert)
        inputs = jnp.where(live_rows, pair_tokens[picked], zero_half)
        gate_pre = jnp.dot(inputs, gate_weight, preferred_element_type=jnp.float32)
        up_pre = jnp.dot(inputs, up_weight, preferred_element_type=jnp.float32)
        active = (jax.nn.silu(gate_pre) * up_pre).astype(jnp.bfloat16)
        produced = jnp.dot(active, down_weight, preferred_element_type=jnp.float32).astype(jnp.bfloat16)
        accumulated = accumulated.at[picked].add(jnp.where(live_rows, produced.astype(jnp.float32), 0.0))
        return accumulated, None

    pair_out, _ = lax.scan(forward_one, jnp.zeros((pair_count, D), jnp.float32), (w_gate, w_up, w_down, expert_list))
    prob_grad = jnp.sum(pair_grads.astype(jnp.float32) * pair_out, axis=1).reshape(row_count, TOP_WIN)
    prob_full = jnp.concatenate([prob_grad, jnp.zeros((row_count, TOP - TOP_WIN), jnp.float32)], axis=1)
    grad_logits = probability * (prob_full - jnp.sum(probability * prob_full, axis=1, keepdims=True))
    weighted = (probability[:, :TOP_WIN].reshape(pair_count, 1) * pair_grads.astype(jnp.float32)).astype(jnp.bfloat16)

    def backward_one(accumulated, operand):
        gate_weight, up_weight, down_weight, expert = operand
        picked, live_rows = select_rows(expert)
        inputs = jnp.where(live_rows, pair_tokens[picked], zero_half)
        gate_pre = jnp.dot(inputs, gate_weight, preferred_element_type=jnp.float32)
        up_pre = jnp.dot(inputs, up_weight, preferred_element_type=jnp.float32)
        sigmoid_gate = jax.nn.sigmoid(gate_pre)
        active = (jax.nn.silu(gate_pre) * up_pre).astype(jnp.bfloat16)
        upstream = jnp.where(live_rows, weighted[picked], zero_half)
        grad_active = jnp.dot(upstream, down_weight.T, preferred_element_type=jnp.float32)
        grad_down = jnp.dot(active.T, upstream, preferred_element_type=jnp.float32).astype(jnp.bfloat16)
        grad_gate_pre = (grad_active * up_pre * sigmoid_gate * (1.0 + gate_pre * (1.0 - sigmoid_gate))).astype(jnp.bfloat16)
        grad_up_pre = (grad_active * jax.nn.silu(gate_pre)).astype(jnp.bfloat16)
        grad_gate = jnp.dot(inputs.T, grad_gate_pre, preferred_element_type=jnp.float32).astype(jnp.bfloat16)
        grad_up = jnp.dot(inputs.T, grad_up_pre, preferred_element_type=jnp.float32).astype(jnp.bfloat16)
        grad_pair = (jnp.dot(grad_gate_pre, gate_weight.T, preferred_element_type=jnp.float32)
                     + jnp.dot(grad_up_pre, up_weight.T, preferred_element_type=jnp.float32)).astype(jnp.bfloat16)
        accumulated = accumulated.at[picked].add(jnp.where(live_rows, grad_pair.astype(jnp.float32), 0.0))
        return accumulated, (grad_gate, grad_up, grad_down)

    pair_sum, weight_grads = lax.scan(backward_one, jnp.zeros((pair_count, D), jnp.float32), (w_gate, w_up, w_down, expert_list))
    grad_tokens = jnp.sum(pair_sum.reshape(row_count, TOP_WIN, D), axis=1).astype(jnp.bfloat16)
    return grad_tokens, grad_logits, weight_grads[0], weight_grads[1], weight_grads[2]


def reference(tokens, route_ids, route_logits, grad_out, w_gate, w_up, w_down, drift, outer, momentum, inner_now):
    group_rows = TOK_DEV * N_EXPERT
    grouped = (tokens.reshape(N_REPLICA, group_rows, D), route_ids.reshape(N_REPLICA, group_rows, TOP_WIN),
               route_logits.reshape(N_REPLICA, group_rows, TOP), grad_out.reshape(N_REPLICA, group_rows, D),
               w_gate, w_up, w_down)
    results = lax.map(replica_pass, grouped)
    grad_tokens = results[0].reshape(TOKENS, D)
    grad_logits = results[1].reshape(TOKENS, TOP)
    average = jnp.sum(drift, axis=0) / N_REPLICA
    new_momentum = momentum_rate * momentum + average
    new_outer = outer - outer_rate * (average + momentum_rate * new_momentum)
    merged = (mix_rate * inner_now.astype(jnp.float32) + (1.0 - mix_rate) * new_outer[None]).astype(jnp.bfloat16)
    return grad_tokens, grad_logits, results[2], results[3], results[4], new_outer, new_momentum, merged
```

```python
import jax
import jax.numpy as jnp
from jax import lax
from jax.experimental import pallas as pl
from jax.experimental.pallas import tpu as pltpu
from jax.sharding import PartitionSpec as P

MESH = pl.DeviceIdType.MESH
D = 2048
FF = 768
HALF = D // 2
CAP = 24
BLOCKS = 8
ROWS = BLOCKS * CAP
GROUP = 4
GROUP_ROWS = GROUP * CAP
REPLICAS = 16

momentum_rate = 0.9
outer_rate = 0.7
mix_rate = 0.5

OFFSETS = ((1, 0), (3, 0), (1, 1), (3, 1), (2, 0), (2, 1), (0, 1), (0, 0))
OWN = 7


def f32(value):
    return value.astype(jnp.float32)


def to_wire(rows):
    blocks = rows.reshape(-1, CAP, D)
    return jnp.concatenate([blocks[:, :, :HALF], blocks[:, :, HALF:]], axis=1).astype(jnp.bfloat16)


def from_wire(blocks):
    wide = f32(blocks)
    count = wide.shape[0]
    left = wide[:, :CAP, :].reshape(count * CAP, HALF)
    right = wide[:, CAP:, :].reshape(count * CAP, HALF)
    return jnp.concatenate([left, right], axis=1).astype(jnp.bfloat16)


def dot(left, right, left_axis=1, right_axis=0):
    return lax.dot_general(
        left, right, (((left_axis,), (right_axis,)), ((), ())), preferred_element_type=jnp.float32
    )


def exchange_kernel(
    ids_hbm, logits_hbm, tokens_hbm, grads_hbm, gate_hbm, up_hbm, down_hbm, drift_hbm, outer_hbm, momentum_hbm,
    x_out, weighted_out, active_out, dgate_out, dup_out, back_out, select_out, dots_out, average_out, whole_out,
    ids, logits, tokens, grads, gate_w, up_w, down_w, drift_mine, drift_other, outer, momentum,
    token_send, token_recv, weighted_send, weighted_recv, back_send, dots_send, dots_recv,
    core_send, core_recv, y_send, y_recv, z_send, z_recv,
    local_sem, send_sem, recv_sem, core_sems, y_sems, z_sems,
):
    replica = lax.axis_index("replica")
    expert = lax.axis_index("expert")
    my_y, my_zh, my_core = replica // 4, (replica // 2) % 2, replica % 2
    my_x, my_zl = expert // 2, expert % 2

    def peer(dx, dz):
        return (replica, ((my_x + dx) % 4) * 2 + (my_zl + dz) % 2)

    def twin(dy, dzh, dcore):
        return ((((my_y + dy) % 4) * 2 + (my_zh + dzh) % 2) * 2 + (my_core + dcore) % 2, expert)

    core_twin = twin(0, 0, 1)
    z_twin = twin(0, 1, 0)
    y_twins = [twin(dy, 0, 0) for dy in (1, 2, 3)]

    barrier = pltpu.get_barrier_semaphore()
    partners = [peer(*offset) for offset in OFFSETS[:OWN]] + y_twins + [core_twin, z_twin]
    for partner in partners:
        pl.semaphore_signal(barrier, inc=1, device_id=partner, device_id_type=MESH)

    loads = {}
    pairs = dict(
        ids=(ids_hbm, ids), tokens=(tokens_hbm, tokens), logits=(logits_hbm, logits), grads=(grads_hbm, grads),
        other0=(drift_hbm.at[0, :, 1 - my_core], drift_other.at[:, 0]),
        other1=(drift_hbm.at[1, :, 1 - my_core], drift_other.at[:, 1]),
        mine0=(drift_hbm.at[0, :, my_core], drift_mine.at[:, 0]),
        mine1=(drift_hbm.at[1, :, my_core], drift_mine.at[:, 1]),
        gate=(gate_hbm, gate_w), up=(up_hbm, up_w), down=(down_hbm, down_w),
        outer=(outer_hbm, outer), momentum=(momentum_hbm, momentum),
    )
    for number, (name, (source, target)) in enumerate(pairs.items()):
        loads[name] = pltpu.make_async_copy(source, target, local_sem.at[number])
        loads[name].start()

    def remote(source, target, sems, device):
        return pltpu.make_async_remote_copy(
            src_ref=source, dst_ref=target, send_sem=sems[0], recv_sem=sems[1], device_id=device, device_id_type=MESH
        )

    def spread(send, recv, kind, forward):
        copies = []
        for block, (dx, dz) in enumerate(OFFSETS[:OWN]):
            device = peer(dx, dz) if forward else peer(-dx % 4, -dz % 2)
            sems = (send_sem.at[kind, block], recv_sem.at[kind, block])
            copies.append(remote(send.at[block], recv.at[block], sems, device))
        return copies

    token_copies = spread(token_send, token_recv, 0, True)
    weighted_copies = spread(weighted_send, weighted_recv, 1, True)
    back_copies = spread(back_send, back_out, 2, False)
    dots_copies = spread(dots_send, dots_recv, 3, False)

    loads["ids"].wait()
    id_row = ids[...]
    row = lax.broadcasted_iota(jnp.int32, (16, 128), 0)
    named = jnp.full((16, 128), -1, jnp.int32)
    for block, offset in enumerate(OFFSETS):
        named = jnp.where(row == block, peer(*offset)[1], named)
    onehot = jnp.where(named == id_row, 1.0, 0.0)
    before_mask = lax.broadcasted_iota(jnp.int32, (128, 128), 0) < lax.broadcasted_iota(jnp.int32, (128, 128), 1)
    before = dot(onehot.astype(jnp.bfloat16), jnp.where(before_mask, 1.0, 0.0).astype(jnp.bfloat16))
    slot = jnp.sum(onehot * (before + f32(row) * CAP), axis=0, keepdims=True)
    slot_row = lax.broadcasted_iota(jnp.int32, (ROWS, 128), 0)
    select = jnp.where(slot_row == slot.astype(jnp.int32), 1.0, 0.0).astype(jnp.bfloat16)
    select_out[...] = select

    def place(part, values, send, recv):
        first = part * GROUP
        wire = to_wire(dot(select[first * CAP : (first + GROUP) * CAP], values))
        if part == 0:
            send[0:GROUP] = wire
        else:
            send[GROUP:OWN] = wire[: OWN - GROUP]
            recv[OWN] = wire[OWN - GROUP]

    loads["tokens"].wait()
    values = tokens[...]
    place(0, values, token_send, token_recv)
    pl.semaphore_wait(barrier, len(partners))
    for copy in token_copies[:GROUP]:
        copy.start()

    loads["logits"].wait()
    scores = logits[...]
    powers = jnp.exp(scores - jnp.max(scores, axis=0, keepdims=True))
    probability = powers / jnp.sum(powers, axis=0, keepdims=True)
    column = jnp.transpose(jnp.broadcast_to(probability[0:1, :], (128, 128)))
    loads["grads"].wait()
    weighted = (f32(grads[...]) * jnp.concatenate([column] * (D // 128), axis=1)).astype(jnp.bfloat16)
    place(0, weighted, weighted_send, weighted_recv)
    for copy in weighted_copies[:GROUP]:
        copy.start()
    place(1, values, token_send, token_recv)
    for copy in token_copies[GROUP:]:
        copy.start()
    place(1, weighted, weighted_send, weighted_recv)
    for copy in weighted_copies[GROUP:]:
        copy.start()

    core_sum = remote(core_send, core_recv, (core_sems.at[0], core_sems.at[1]), core_twin)
    loads["other0"].wait()
    loads["other1"].wait()
    core_send[...] = drift_other[...].astype(jnp.bfloat16)
    core_sum.start()
    loads["mine0"].wait()
    loads["mine1"].wait()
    core_sum.wait()
    y_send[...] = (drift_mine[...] + f32(core_recv[...])).astype(jnp.bfloat16)
    y_sum = []
    for step in range(3):
        there = (my_y + step + 1) % 4
        copy = remote(
            y_send.at[pl.ds(there * 2, 2)], y_recv.at[step], (y_sems.at[0, step], y_sems.at[1, step]), y_twins[step]
        )
        copy.start()
        y_sum.append(copy)

    def front(part):
        first = part * GROUP
        rows = pl.ds(first * CAP, GROUP_ROWS)
        if part == 0:
            for copy in token_copies[:GROUP]:
                copy.wait_recv()
        inputs = from_wire(token_recv[first : first + GROUP])
        x_out[rows, :] = inputs
        if part == 0:
            loads["gate"].wait()
            loads["up"].wait()
        gate = dot(inputs, gate_w[...])
        up = dot(inputs, up_w[...])
        sigmoid = 1.0 / (1.0 + jnp.exp(-gate))
        silu = gate * sigmoid
        active = silu * up
        active_out[rows, :] = active.astype(jnp.bfloat16)
        if part == 0:
            for copy in weighted_copies[:GROUP]:
                copy.wait_recv()
        upstream = from_wire(weighted_recv[first : first + GROUP])
        weighted_out[rows, :] = upstream
        if part == 0:
            loads["down"].wait()
        grad_active = dot(upstream, down_w[...], 1, 1)
        scalars = jnp.sum(grad_active * active, axis=1, keepdims=True)
        dgate = (grad_active * up * sigmoid * (1.0 + gate * (1.0 - sigmoid))).astype(jnp.bfloat16)
        dup = (grad_active * silu).astype(jnp.bfloat16)
        dgate_out[rows, :] = dgate
        dup_out[rows, :] = dup
        lane = lax.broadcasted_iota(jnp.int32, (8, 128), 1)
        for block in range(GROUP):
            eights = [jnp.broadcast_to(scalars[block * CAP + 8 * i : block * CAP + 8 * i + 8], (8, 128)) for i in range(3)]
            packed = jnp.where(lane < 32, eights[0], jnp.where(lane < 64, eights[1], eights[2]))
            if first + block == OWN:
                dots_recv[OWN] = packed
            else:
                dots_send[first + block] = packed
        wire = to_wire(dot(dgate, gate_w[...], 1, 1) + dot(dup, up_w[...], 1, 1))
        if part == 0:
            back_send[0:GROUP] = wire
        else:
            back_send[GROUP:OWN] = wire[: OWN - GROUP]
            back_out[OWN] = wire[OWN - GROUP]

    front(0)
    for copy in token_copies[GROUP:] + weighted_copies[GROUP:]:
        copy.wait_recv()
    for copy in back_copies[:GROUP] + dots_copies[:GROUP]:
        copy.start()

    for copy in y_sum:
        copy.wait()
    mine = pl.ds(my_y * 2, 2)
    y_total = drift_mine[mine] + f32(core_recv[mine])
    for step in range(3):
        y_total += f32(y_recv[step])
    z_send[...] = y_total.astype(jnp.bfloat16)
    z_sum = remote(z_send.at[1 - my_zh], z_recv, (z_sems.at[0], z_sems.at[1]), z_twin)
    z_sum.start()
    near = jnp.where(my_zh == 0, y_total[0], y_total[1])
    z_sum.wait()
    average = (near + f32(z_recv[...])) / REPLICAS
    average_out[...] = average
    loads["outer"].wait()
    loads["momentum"].wait()
    moment = momentum_rate * momentum[...] + average
    stepped = outer[...] - outer_rate * (average + momentum_rate * moment)
    whole_out[my_core, my_y, my_zh] = stepped.astype(jnp.bfloat16)
    piece = whole_out.at[my_core, my_y, my_zh]
    z_gather = remote(piece, piece, (z_sems.at[2], z_sems.at[3]), z_twin)
    z_gather.start()

    front(1)
    for copy in back_copies[GROUP:] + dots_copies[GROUP:]:
        copy.start()

    z_gather.wait()
    y_gather = []
    for step in range(3):
        piece = whole_out.at[my_core, my_y]
        copy = remote(piece, piece, (y_sems.at[2, step], y_sems.at[3, step]), y_twins[step])
        copy.start()
        y_gather.append(copy)
    for copy in y_gather:
        copy.wait()
    piece = whole_out.at[my_core]
    core_gather = remote(piece, piece, (core_sems.at[2], core_sems.at[3]), core_twin)
    core_gather.start()

    for copy in token_copies + weighted_copies:
        copy.wait_send()
    for copy in dots_copies:
        copy.wait()
    for block in range(BLOCKS):
        for i in range(3):
            start = block * CAP + 8 * i
            dots_out[start : start + 8, :] = jnp.broadcast_to(dots_recv[block][:, 32 * i : 32 * i + 1], (8, 128))
    for copy in back_copies:
        copy.wait()
    core_gather.wait()


def exchange(ids, logits, tokens, grads, w_gate, w_up, w_down, drift, outer, momentum):
    bf16, wide = jnp.bfloat16, jnp.float32
    anywhere = pl.BlockSpec(memory_space=pl.ANY)
    inside = pl.BlockSpec(memory_space=pltpu.VMEM)
    outs = [
        ((ROWS, D), bf16), ((ROWS, D), bf16), ((ROWS, FF), bf16), ((ROWS, FF), bf16), ((ROWS, FF), bf16),
        ((BLOCKS, 2 * CAP, HALF), bf16), ((ROWS, 128), bf16), ((ROWS, 128), wide),
        ((2, 128, 128), wide), ((2, 4, 2, 2, 128, 128), bf16),
    ]
    wire = pltpu.VMEM((BLOCKS, 2 * CAP, HALF), bf16)
    dots = pltpu.VMEM((BLOCKS, 8, 128), wide)
    dma = pltpu.SemaphoreType.DMA
    return pl.pallas_call(
        exchange_kernel,
        out_shape=[jax.ShapeDtypeStruct(*out) for out in outs],
        in_specs=[anywhere] * 10,
        out_specs=[inside] * len(outs),
        scratch_shapes=[
            pltpu.VMEM((1, 128), jnp.int32), pltpu.VMEM((8, 128), wide),
            pltpu.VMEM((128, D), bf16), pltpu.VMEM((128, D), bf16),
            pltpu.VMEM((D, FF), bf16), pltpu.VMEM((D, FF), bf16), pltpu.VMEM((FF, D), bf16),
            pltpu.VMEM((8, 2, 128, 128), wide), pltpu.VMEM((8, 2, 128, 128), wide),
            pltpu.VMEM((2, 128, 128), wide), pltpu.VMEM((2, 128, 128), wide),
            wire, wire, wire, wire, wire, dots, dots,
            pltpu.VMEM((8, 2, 128, 128), bf16), pltpu.VMEM((8, 2, 128, 128), bf16),
            pltpu.VMEM((8, 2, 128, 128), bf16), pltpu.VMEM((3, 2, 2, 128, 128), bf16),
            pltpu.VMEM((2, 2, 128, 128), bf16), pltpu.VMEM((2, 128, 128), bf16),
            dma((13,)), dma((4, OWN)), dma((4, OWN)), dma((4,)), dma((4, 3)), dma((4,)),
        ],
        compiler_params=pltpu.CompilerParams(
            collective_id=0, has_side_effects=True, vmem_limit_bytes=44 << 20
        ),
        cost_estimate=pl.CostEstimate(flops=5 * 2 * ROWS * D * FF, bytes_accessed=16 << 20, transcendentals=ROWS * FF),
    )(ids, logits, tokens, grads, w_gate, w_up, w_down, drift, outer, momentum)


STEPS = 4


def finish_kernel(
    x, weighted, active, dgate, dup, back, select, dots, average, whole, logits, outer, momentum, inner,
    grad_tokens, grad_logits, grad_gate, grad_up, grad_down, new_outer, new_momentum, merged,
):
    step = pl.program_id(0)
    grad_gate[...] = dot(x[...], dgate[...], 0, 0).astype(jnp.bfloat16)
    grad_up[...] = dot(x[...], dup[...], 0, 0).astype(jnp.bfloat16)
    grad_down[...] = dot(active[...], weighted[...], 0, 0).astype(jnp.bfloat16)
    for layer in range(2):
        for zh in range(2):
            for core in range(2):
                rows = pl.ds((zh * 2 + core) * 128, 128)
                merged[layer, rows, :] = (
                    mix_rate * f32(inner[layer, rows, :]) + (1.0 - mix_rate) * f32(whole[core, 0, zh, layer])
                ).astype(jnp.bfloat16)

    @pl.when(step == 0)
    def _():
        grad_tokens[...] = dot(select[...], from_wire(back[...]), 0, 0).astype(jnp.bfloat16)
        scores = logits[...]
        powers = jnp.exp(scores - jnp.max(scores, axis=0, keepdims=True))
        probability = powers / jnp.sum(powers, axis=0, keepdims=True)
        scalar = jnp.sum(f32(select[...]) * dots[...], axis=0, keepdims=True)
        first = lax.broadcasted_iota(jnp.int32, (8, 128), 0) == 0
        grad_logits[...] = jnp.where(first, scalar * (1.0 - probability), -probability * scalar)
        moment = momentum_rate * momentum[...] + average[...]
        new_momentum[...] = moment
        new_outer[...] = outer[...] - outer_rate * (average[...] + momentum_rate * moment)


def finish(x, weighted, active, dgate, dup, back, select, dots, average, whole, logits, outer, momentum, inner):
    bf16, wide = jnp.bfloat16, jnp.float32

    def fixed(shape):
        return pl.BlockSpec(shape, lambda i: (0,) * len(shape))

    x_cols, rows = D // STEPS, D // STEPS
    return pl.pallas_call(
        finish_kernel,
        grid=(STEPS,),
        out_shape=[
            jax.ShapeDtypeStruct((128, D), bf16), jax.ShapeDtypeStruct((8, 128), wide),
            jax.ShapeDtypeStruct((D, FF), bf16), jax.ShapeDtypeStruct((D, FF), bf16),
            jax.ShapeDtypeStruct((FF, D), bf16), jax.ShapeDtypeStruct((2, 128, 128), wide),
            jax.ShapeDtypeStruct((2, 128, 128), wide), jax.ShapeDtypeStruct((2, D, 128), bf16),
        ],
        in_specs=[
            pl.BlockSpec((ROWS, x_cols), lambda i: (0, i)), pl.BlockSpec((ROWS, x_cols), lambda i: (0, i)),
            fixed((ROWS, FF)), fixed((ROWS, FF)), fixed((ROWS, FF)),
            fixed((BLOCKS, 2 * CAP, HALF)), fixed((ROWS, 128)), fixed((ROWS, 128)), fixed((2, 128, 128)),
            pl.BlockSpec((2, 1, 2, 2, 128, 128), lambda i: (0, i, 0, 0, 0, 0)),
            fixed((8, 128)), fixed((2, 128, 128)), fixed((2, 128, 128)),
            pl.BlockSpec((2, rows, 128), lambda i: (0, i, 0)),
        ],
        out_specs=[
            fixed((128, D)), fixed((8, 128)),
            pl.BlockSpec((x_cols, FF), lambda i: (i, 0)), pl.BlockSpec((x_cols, FF), lambda i: (i, 0)),
            pl.BlockSpec((FF, x_cols), lambda i: (0, i)), fixed((2, 128, 128)), fixed((2, 128, 128)),
            pl.BlockSpec((2, rows, 128), lambda i: (0, i, 0)),
        ],
        compiler_params=pltpu.CompilerParams(vmem_limit_bytes=44 << 20),
        cost_estimate=pl.CostEstimate(flops=3 * 2 * ROWS * D * FF, bytes_accessed=18 << 20, transcendentals=1024),
    )(x, weighted, active, dgate, dup, back, select, dots, average, whole, logits, outer, momentum, inner)


def body(tokens, route_ids, route_logits, grad_out, w_gate, w_up, w_down, drift, outer, momentum, inner_now):
    logits = route_logits.T
    sent = exchange(
        route_ids.reshape(1, 128), logits, tokens, grad_out, w_gate[0, 0], w_up[0, 0], w_down[0, 0],
        drift.reshape(2, 8, 2, 128, 128), outer, momentum,
    )
    grad_tokens, grad_logits, grad_gate, grad_up, grad_down, new_outer, new_momentum, merged = finish(
        *sent, logits, outer, momentum, inner_now[0]
    )
    return (
        grad_tokens, grad_logits.T, grad_gate[None, None], grad_up[None, None], grad_down[None, None],
        new_outer, new_momentum, merged[None],
    )


def solution(mesh):
    both = P(("replica", "expert"), None)
    pair = P("replica", "expert", None, None)
    part = P("replica", None, None, "expert")
    shard = P(None, "replica", "expert")
    in_specs = (both, both, both, both, pair, pair, pair, part, shard, shard, part)
    out_specs = (both, both, pair, pair, pair, shard, shard, part)
    return jax.shard_map(body, mesh=mesh, in_specs=in_specs, out_specs=out_specs, check_vma=False)
```

```python
import jax
import jax.numpy as jnp
from jax import lax
from jax.experimental import pallas as pl
from jax.experimental.pallas import tpu as pltpu
from jax.sharding import PartitionSpec as P

MESH = pl.DeviceIdType.MESH
D = 2048
FF = 768
HALF = D // 2
CAP = 24
BLOCKS = 8
ROWS = BLOCKS * CAP
GROUP = 4
GROUP_ROWS = GROUP * CAP
REPLICAS = 16

momentum_rate = 0.9
outer_rate = 0.7
mix_rate = 0.5

OFFSETS = ((1, 0), (3, 0), (1, 1), (3, 1), (2, 0), (2, 1), (0, 1), (0, 0))
OWN = 7


def f32(value):
    return value.astype(jnp.float32)


def to_wire(rows):
    blocks = rows.reshape(-1, CAP, D)
    return jnp.concatenate([blocks[:, :, :HALF], blocks[:, :, HALF:]], axis=1).astype(jnp.bfloat16)


def from_wire(blocks):
    wide = f32(blocks)
    count = wide.shape[0]
    left = wide[:, :CAP, :].reshape(count * CAP, HALF)
    right = wide[:, CAP:, :].reshape(count * CAP, HALF)
    return jnp.concatenate([left, right], axis=1).astype(jnp.bfloat16)


def dot(left, right, left_axis=1, right_axis=0):
    return lax.dot_general(
        left, right, (((left_axis,), (right_axis,)), ((), ())), preferred_element_type=jnp.float32
    )


def exchange_kernel(
    ids_hbm, logits_hbm, tokens_hbm, grads_hbm, gate_hbm, up_hbm, down_hbm, drift_hbm, outer_hbm, momentum_hbm,
    grad_gate_out, grad_up_out, grad_down_out, back_out, select_out, dots_out, average_out, whole_out,
    x_keep, weighted_keep, active_keep, dgate_keep, dup_keep, y_total, ids, logits, tokens, grads, gate_w, up_w, down_w, drift_mine, drift_other, outer, momentum,
    token_send, token_recv, weighted_send, weighted_recv, back_send, dots_send, dots_recv,
    core_send, core_recv, y_send, y_recv, z_send, z_recv,
    local_sem, send_sem, recv_sem, core_sems, y_sems, z_sems,
):
    replica = lax.axis_index("replica")
    expert = lax.axis_index("expert")
    my_y, my_zh, my_core = replica // 4, (replica // 2) % 2, replica % 2
    my_x, my_zl = expert // 2, expert % 2

    def peer(dx, dz):
        return (replica, ((my_x + dx) % 4) * 2 + (my_zl + dz) % 2)

    def twin(dy, dzh, dcore):
        return ((((my_y + dy) % 4) * 2 + (my_zh + dzh) % 2) * 2 + (my_core + dcore) % 2, expert)

    core_twin = twin(0, 0, 1)
    z_twin = twin(0, 1, 0)
    y_twins = [twin(dy, 0, 0) for dy in (1, 2, 3)]

    barrier = pltpu.get_barrier_semaphore()
    partners = [peer(*offset) for offset in OFFSETS[:OWN]] + y_twins + [core_twin, z_twin]
    for partner in partners:
        pl.semaphore_signal(barrier, inc=1, device_id=partner, device_id_type=MESH)

    loads = {}
    pairs = dict(
        ids=(ids_hbm, ids), tokens=(tokens_hbm, tokens), logits=(logits_hbm, logits), grads=(grads_hbm, grads),
        other0=(drift_hbm.at[0, :, 1 - my_core], drift_other.at[:, 0]),
        other1=(drift_hbm.at[1, :, 1 - my_core], drift_other.at[:, 1]),
        mine0=(drift_hbm.at[0, :, my_core], drift_mine.at[:, 0]),
        mine1=(drift_hbm.at[1, :, my_core], drift_mine.at[:, 1]),
        gate=(gate_hbm, gate_w), up=(up_hbm, up_w), down=(down_hbm, down_w),
        outer=(outer_hbm, outer), momentum=(momentum_hbm, momentum),
    )
    for number, (name, (source, target)) in enumerate(pairs.items()):
        loads[name] = pltpu.make_async_copy(source, target, local_sem.at[number])
        loads[name].start()

    def remote(source, target, sems, device):
        return pltpu.make_async_remote_copy(
            src_ref=source, dst_ref=target, send_sem=sems[0], recv_sem=sems[1], device_id=device, device_id_type=MESH
        )

    def spread(send, recv, kind, forward):
        copies = []
        for block, (dx, dz) in enumerate(OFFSETS[:OWN]):
            device = peer(dx, dz) if forward else peer(-dx % 4, -dz % 2)
            sems = (send_sem.at[kind, block], recv_sem.at[kind, block])
            copies.append(remote(send.at[block], recv.at[block], sems, device))
        return copies

    token_copies = spread(token_send, token_recv, 0, True)
    weighted_copies = spread(weighted_send, weighted_recv, 1, True)
    back_copies = spread(back_send, back_out, 2, False)
    dots_copies = spread(dots_send, dots_recv, 3, False)

    loads["ids"].wait()
    id_row = ids[...]
    row = lax.broadcasted_iota(jnp.int32, (16, 128), 0)
    named = jnp.full((16, 128), -1, jnp.int32)
    for block, offset in enumerate(OFFSETS):
        named = jnp.where(row == block, peer(*offset)[1], named)
    onehot = jnp.where(named == id_row, 1.0, 0.0)
    before_mask = lax.broadcasted_iota(jnp.int32, (128, 128), 0) < lax.broadcasted_iota(jnp.int32, (128, 128), 1)
    before = dot(onehot.astype(jnp.bfloat16), jnp.where(before_mask, 1.0, 0.0).astype(jnp.bfloat16))
    slot = jnp.sum(onehot * (before + f32(row) * CAP), axis=0, keepdims=True)
    slot_row = lax.broadcasted_iota(jnp.int32, (ROWS, 128), 0)
    select = jnp.where(slot_row == slot.astype(jnp.int32), 1.0, 0.0).astype(jnp.bfloat16)
    select_out[...] = select

    def place(part, values, send, recv):
        first = part * GROUP
        wire = to_wire(dot(select[first * CAP : (first + GROUP) * CAP], values))
        if part == 0:
            send[0:GROUP] = wire
        else:
            send[GROUP:OWN] = wire[: OWN - GROUP]
            recv[OWN] = wire[OWN - GROUP]

    loads["tokens"].wait()
    values = tokens[...]
    place(0, values, token_send, token_recv)
    pl.semaphore_wait(barrier, len(partners))
    for copy in token_copies[:GROUP]:
        copy.start()

    core_sum = remote(core_send, core_recv, (core_sems.at[0], core_sems.at[1]), core_twin)
    loads["other0"].wait()
    loads["other1"].wait()
    core_send[...] = drift_other[...].astype(jnp.bfloat16)
    core_sum.start()

    loads["logits"].wait()
    scores = logits[...]
    powers = jnp.exp(scores - jnp.max(scores, axis=0, keepdims=True))
    probability = powers / jnp.sum(powers, axis=0, keepdims=True)
    column = jnp.transpose(jnp.broadcast_to(probability[0:1, :], (128, 128)))
    loads["grads"].wait()
    weighted = (f32(grads[...]) * jnp.concatenate([column] * (D // 128), axis=1)).astype(jnp.bfloat16)
    place(0, weighted, weighted_send, weighted_recv)
    for copy in weighted_copies[:GROUP]:
        copy.start()
    place(1, values, token_send, token_recv)
    for copy in token_copies[GROUP:]:
        copy.start()
    place(1, weighted, weighted_send, weighted_recv)
    weighted_copies[GROUP].start()
    weighted_copies[GROUP + 1].start()

    loads["mine0"].wait()
    loads["mine1"].wait()
    core_sum.wait()
    y_send[...] = (drift_mine[...] + f32(core_recv[...])).astype(jnp.bfloat16)
    y_sum = []
    for step in range(3):
        there = (my_y + step + 1) % 4
        copy = remote(
            y_send.at[pl.ds(there * 2, 2)], y_recv.at[step], (y_sems.at[0, step], y_sems.at[1, step]), y_twins[step]
        )
        copy.start()
        y_sum.append(copy)

    def front_in(part):
        first = part * GROUP
        rows = pl.ds(first * CAP, GROUP_ROWS)
        count = GROUP if part == 0 else OWN - GROUP
        for copy in token_copies[first : first + count]:
            copy.wait_recv()
        inputs = from_wire(token_recv[first : first + GROUP])
        x_keep[rows, :] = inputs
        if part == 0:
            loads["gate"].wait()
            loads["up"].wait()
        gate = dot(inputs, gate_w[...])
        up = dot(inputs, up_w[...])
        sigmoid = 1.0 / (1.0 + jnp.exp(-gate))
        silu = gate * sigmoid
        active = silu * up
        active_keep[rows, :] = active.astype(jnp.bfloat16)
        return inputs, gate, up, sigmoid, silu, active

    def front_out(part, kept):
        inputs, gate, up, sigmoid, silu, active = kept
        first = part * GROUP
        rows = pl.ds(first * CAP, GROUP_ROWS)
        count = GROUP if part == 0 else OWN - GROUP
        for copy in weighted_copies[first : first + count]:
            copy.wait_recv()
        upstream = from_wire(weighted_recv[first : first + GROUP])
        weighted_keep[rows, :] = upstream
        if part == 0:
            loads["down"].wait()
        grad_active = dot(upstream, down_w[...], 1, 1)
        scalars = jnp.sum(grad_active * active, axis=1, keepdims=True)
        dgate = (grad_active * up * sigmoid * (1.0 + gate * (1.0 - sigmoid))).astype(jnp.bfloat16)
        dup = (grad_active * silu).astype(jnp.bfloat16)
        dgate_keep[rows, :] = dgate
        dup_keep[rows, :] = dup
        lane = lax.broadcasted_iota(jnp.int32, (8, 128), 1)
        for block in range(GROUP):
            eights = [jnp.broadcast_to(scalars[block * CAP + 8 * i : block * CAP + 8 * i + 8], (8, 128)) for i in range(3)]
            packed = jnp.where(lane < 32, eights[0], jnp.where(lane < 64, eights[1], eights[2]))
            if first + block == OWN:
                dots_recv[OWN] = packed
            else:
                dots_send[first + block] = packed
        wire = to_wire(dot(dgate, gate_w[...], 1, 1) + dot(dup, up_w[...], 1, 1))
        if part == 0:
            back_send[0:GROUP] = wire
        else:
            back_send[GROUP:OWN] = wire[: OWN - GROUP]
            back_out[OWN] = wire[OWN - GROUP]

    def gather(part, sems, device):
        return remote(part, part, sems, device)

    z_sum = remote(z_send.at[1 - my_zh], z_recv, (z_sems.at[0], z_sems.at[1]), z_twin)
    near = whole_out.at[my_core, my_y, my_zh]
    far = whole_out.at[my_core, my_y, 1 - my_zh]
    z_gather = gather(near, (z_sems.at[2], z_sems.at[3]), z_twin)
    y_near = [gather(near, (y_sems.at[2, step], y_sems.at[3, step]), y_twins[step]) for step in range(3)]
    y_far = [gather(far, (y_sems.at[4, step], y_sems.at[5, step]), y_twins[step]) for step in range(3)]
    core_near = gather(whole_out.at[my_core, :, my_zh], (core_sems.at[2], core_sems.at[3]), core_twin)
    core_far = gather(whole_out.at[my_core, :, 1 - my_zh], (core_sems.at[4], core_sems.at[5]), core_twin)

    def start(copies):
        for copy in copies:
            copy.start()

    def wait(copies):
        for copy in copies:
            copy.wait()

    kept = front_in(0)
    wait(y_sum)
    mine = pl.ds(my_y * 2, 2)
    y_total[...] = drift_mine[mine] + f32(core_recv[mine]) + f32(y_recv[0]) + f32(y_recv[1]) + f32(y_recv[2])
    z_send[...] = y_total[...].astype(jnp.bfloat16)
    z_sum.start()
    start(weighted_copies[GROUP + 2 :])
    front_out(0, kept)
    start(back_copies[:2] + dots_copies[:2])
    kept = front_in(1)
    loads["outer"].wait()
    loads["momentum"].wait()
    z_sum.wait()
    average = (jnp.where(my_zh == 0, y_total[0], y_total[1]) + f32(z_recv[...])) / REPLICAS
    average_out[...] = average
    moment = momentum_rate * momentum[...] + average
    stepped = outer[...] - outer_rate * (average + momentum_rate * moment)
    near[...] = stepped.astype(jnp.bfloat16)
    start([z_gather] + y_near)
    start(back_copies[2:GROUP] + dots_copies[2:GROUP])
    front_out(1, kept)
    start(back_copies[GROUP:] + dots_copies[GROUP:])
    z_gather.wait()
    start(y_far)
    wait(y_near)
    core_near.start()

    def wide_tile(index, carry):
        columns = pl.ds(pl.multiple_of(index * 256, 256), 256)
        inputs = x_keep[:, columns]
        grad_gate_out[columns, :] = dot(inputs, dgate_keep[...], 0, 0).astype(jnp.bfloat16)
        grad_up_out[columns, :] = dot(inputs, dup_keep[...], 0, 0).astype(jnp.bfloat16)
        return carry

    def down_tile(index, carry):
        columns = pl.ds(pl.multiple_of(index * 128, 128), 128)
        grad_down_out[columns, :] = dot(active_keep[:, columns], weighted_keep[...], 0, 0).astype(jnp.bfloat16)
        return carry

    lax.fori_loop(0, D // 256, wide_tile, 0)
    wait(y_far)
    core_far.start()
    lax.fori_loop(0, FF // 128, down_tile, 0)

    for copy in token_copies + weighted_copies:
        copy.wait_send()
    wait(dots_copies)
    for block in range(BLOCKS):
        for i in range(3):
            first = block * CAP + 8 * i
            dots_out[first : first + 8, :] = jnp.broadcast_to(dots_recv[block][:, 32 * i : 32 * i + 1], (8, 128))
    wait(back_copies)
    wait([core_near, core_far])


def exchange(ids, logits, tokens, grads, w_gate, w_up, w_down, drift, outer, momentum):
    bf16, wide = jnp.bfloat16, jnp.float32
    anywhere = pl.BlockSpec(memory_space=pltpu.HBM)
    inside = pl.BlockSpec(memory_space=pltpu.VMEM)
    outs = [
        ((D, FF), bf16), ((D, FF), bf16), ((FF, D), bf16),
        ((BLOCKS, 2 * CAP, HALF), bf16), ((ROWS, 128), bf16), ((ROWS, 128), wide),
        ((2, 128, 128), wide), ((2, 4, 2, 2, 128, 128), bf16),
    ]
    wire = pltpu.VMEM((BLOCKS, 2 * CAP, HALF), bf16)
    dots = pltpu.VMEM((BLOCKS, 8, 128), wide)
    dma = pltpu.SemaphoreType.DMA
    return pl.pallas_call(
        exchange_kernel,
        out_shape=[jax.ShapeDtypeStruct(*out) for out in outs],
        in_specs=[anywhere] * 10,
        out_specs=[inside] * len(outs),
        scratch_shapes=[
            pltpu.VMEM((ROWS, D), bf16), pltpu.VMEM((ROWS, D), bf16), pltpu.VMEM((ROWS, FF), bf16),
            pltpu.VMEM((ROWS, FF), bf16), pltpu.VMEM((ROWS, FF), bf16), pltpu.VMEM((2, 2, 128, 128), wide),
            pltpu.VMEM((1, 128), jnp.int32), pltpu.VMEM((8, 128), wide),
            pltpu.VMEM((128, D), bf16), pltpu.VMEM((128, D), bf16),
            pltpu.VMEM((D, FF), bf16), pltpu.VMEM((D, FF), bf16), pltpu.VMEM((FF, D), bf16),
            pltpu.VMEM((8, 2, 128, 128), wide), pltpu.VMEM((8, 2, 128, 128), wide),
            pltpu.VMEM((2, 128, 128), wide), pltpu.VMEM((2, 128, 128), wide),
            wire, wire, wire, wire, wire, dots, dots,
            pltpu.VMEM((8, 2, 128, 128), bf16), pltpu.VMEM((8, 2, 128, 128), bf16),
            pltpu.VMEM((8, 2, 128, 128), bf16), pltpu.VMEM((3, 2, 2, 128, 128), bf16),
            pltpu.VMEM((2, 2, 128, 128), bf16), pltpu.VMEM((2, 128, 128), bf16),
            dma((13,)), dma((4, OWN)), dma((4, OWN)), dma((6,)), dma((6, 3)), dma((4,)),
        ],
        compiler_params=pltpu.CompilerParams(
            collective_id=0, has_side_effects=True, vmem_limit_bytes=32 << 20
        ),
        cost_estimate=pl.CostEstimate(flops=5 * 2 * ROWS * D * FF, bytes_accessed=16 << 20, transcendentals=ROWS * FF),
    )(*[pltpu.with_memory_space_constraint(a, pltpu.HBM) for a in (ids, logits, tokens, grads, w_gate, w_up, w_down, drift, outer, momentum)])


def finish_kernel(
    gate_in, up_in, down_in, back, select, dots, average, whole, logits, outer, momentum, inner,
    grad_tokens, grad_logits, grad_gate, grad_up, grad_down, new_outer, new_momentum, merged,
    tokens_keep, logits_keep, outer_keep, momentum_keep, merged_keep, sems,
):
    copies = []

    def put(source, target):
        copies.append(pltpu.make_async_copy(source, target, sems.at[len(copies)]))
        copies[-1].start()

    for source, target in ((gate_in, grad_gate), (up_in, grad_up), (down_in, grad_down)):
        size = source.shape[0] // 4
        for part in range(4):
            put(source.at[pl.ds(part * size, size)], target.at[pl.ds(part * size, size)])
    grad_tokens_rows = dot(select[...], from_wire(back[...]), 0, 0).astype(jnp.bfloat16)
    tokens_keep[...] = grad_tokens_rows
    put(tokens_keep, grad_tokens)
    moment = momentum_rate * momentum[...] + average[...]
    momentum_keep[...] = moment
    put(momentum_keep, new_momentum)
    outer_keep[...] = outer[...] - outer_rate * (average[...] + momentum_rate * moment)
    put(outer_keep, new_outer)
    scores = logits[...]
    powers = jnp.exp(scores - jnp.max(scores, axis=0, keepdims=True))
    probability = powers / jnp.sum(powers, axis=0, keepdims=True)
    scalar = jnp.sum(f32(select[...]) * dots[...], axis=0, keepdims=True)
    first = lax.broadcasted_iota(jnp.int32, (8, 128), 0) == 0
    logits_keep[...] = jnp.where(first, scalar * (1.0 - probability), -probability * scalar)
    put(logits_keep, grad_logits)
    for y in range(4):
        for zh in range(2):
            for core in range(2):
                rows = pl.ds(((y * 2 + zh) * 2 + core) * 128, 128)
                for layer in range(2):
                    merged_keep[layer, rows, :] = (
                        mix_rate * f32(inner[layer, rows, :]) + (1.0 - mix_rate) * f32(whole[core, y, zh, layer])
                    ).astype(jnp.bfloat16)
    put(merged_keep, merged)
    for copy in copies:
        copy.wait()


def finish(gate_in, up_in, down_in, back, select, dots, average, whole, logits, outer, momentum, inner):
    bf16, wide = jnp.bfloat16, jnp.float32
    anywhere = pl.BlockSpec(memory_space=pl.ANY)
    inside = pl.BlockSpec(memory_space=pltpu.VMEM)
    return pl.pallas_call(
        finish_kernel,
        out_shape=[
            jax.ShapeDtypeStruct((128, D), bf16), jax.ShapeDtypeStruct((8, 128), wide),
            jax.ShapeDtypeStruct((D, FF), bf16), jax.ShapeDtypeStruct((D, FF), bf16),
            jax.ShapeDtypeStruct((FF, D), bf16), jax.ShapeDtypeStruct((2, 128, 128), wide),
            jax.ShapeDtypeStruct((2, 128, 128), wide), jax.ShapeDtypeStruct((2, D, 128), bf16),
        ],
        in_specs=[anywhere] * 3 + [inside] * 9,
        out_specs=[anywhere] * 8,
        scratch_shapes=[
            pltpu.VMEM((128, D), bf16), pltpu.VMEM((8, 128), wide), pltpu.VMEM((2, 128, 128), wide),
            pltpu.VMEM((2, 128, 128), wide), pltpu.VMEM((2, D, 128), bf16), pltpu.SemaphoreType.DMA((17,)),
        ],
        compiler_params=pltpu.CompilerParams(vmem_limit_bytes=20 << 20),
        cost_estimate=pl.CostEstimate(flops=2 * ROWS * D * 128, bytes_accessed=22 << 20, transcendentals=1024),
    )(gate_in, up_in, down_in, back, select, dots, average, whole, logits, outer, momentum, inner)


def body(tokens, route_ids, route_logits, grad_out, w_gate, w_up, w_down, drift, outer, momentum, inner_now):
    logits = route_logits.T
    sent = exchange(
        route_ids.reshape(1, 128), logits, tokens, grad_out, w_gate[0, 0], w_up[0, 0], w_down[0, 0],
        drift.reshape(2, 8, 2, 128, 128), outer, momentum,
    )
    grad_tokens, grad_logits, grad_gate, grad_up, grad_down, new_outer, new_momentum, merged = finish(
        *sent, logits, outer, momentum, inner_now[0]
    )
    return (
        grad_tokens, grad_logits.T, grad_gate[None, None], grad_up[None, None], grad_down[None, None],
        new_outer, new_momentum, merged[None],
    )


def solution(mesh):
    both = P(("replica", "expert"), None)
    pair = P("replica", "expert", None, None)
    part = P("replica", None, None, "expert")
    shard = P(None, "replica", "expert")
    in_specs = (both, both, both, both, pair, pair, pair, part, shard, shard, part)
    out_specs = (both, both, pair, pair, pair, shard, shard, part)
    return jax.shard_map(body, mesh=mesh, in_specs=in_specs, out_specs=out_specs, check_vma=False)
```

```python
import jax
import jax.numpy as jnp
from jax import lax
from jax.experimental import pallas as pl
from jax.experimental.pallas import tpu as pltpu
from jax.sharding import PartitionSpec as P

MESH = pl.DeviceIdType.MESH
D = 2048
FF = 768
HALF = D // 2
CAP = 24
BLOCKS = 8
ROWS = BLOCKS * CAP
GROUP = 4
GROUP_ROWS = GROUP * CAP
REPLICAS = 16

momentum_rate = 0.9
outer_rate = 0.7
mix_rate = 0.5

OFFSETS = ((1, 0), (3, 0), (1, 1), (3, 1), (2, 1), (2, 0), (0, 1), (0, 0))
OWN = 7


def f32(value):
    return value.astype(jnp.float32)


def to_wire(rows):
    blocks = rows.reshape(-1, CAP, D)
    return jnp.concatenate([blocks[:, :, :HALF], blocks[:, :, HALF:]], axis=1).astype(jnp.bfloat16)


def from_wire(blocks):
    wide = f32(blocks)
    count = wide.shape[0]
    left = wide[:, :CAP, :].reshape(count * CAP, HALF)
    right = wide[:, CAP:, :].reshape(count * CAP, HALF)
    return jnp.concatenate([left, right], axis=1).astype(jnp.bfloat16)


def dot(left, right, left_axis=1, right_axis=0):
    return lax.dot_general(
        left, right, (((left_axis,), (right_axis,)), ((), ())), preferred_element_type=jnp.float32
    )


def exchange_kernel(
    ids_hbm, logits_hbm, tokens_hbm, grads_hbm, gate_hbm, up_hbm, down_hbm, drift_hbm, outer_hbm, momentum_hbm,
    grad_gate_out, grad_up_out, grad_down_out, back_out, select_out, dots_out, average_out, whole_out,
    x_keep, weighted_keep, active_keep, dgate_keep, dup_keep, y_total, ids, logits, tokens, grads, gate_w, up_w, down_w, drift_mine, drift_other, outer, momentum,
    token_send, token_recv, weighted_send, weighted_recv, back_send, dots_send, dots_recv,
    core_send, core_recv, y_send, y_recv, z_send, z_recv,
    local_sem, send_sem, recv_sem, core_sems, y_sems, z_sems,
):
    replica = lax.axis_index("replica")
    expert = lax.axis_index("expert")
    my_y, my_zh, my_core = replica // 4, (replica // 2) % 2, replica % 2
    my_x, my_zl = expert // 2, expert % 2

    def peer(dx, dz):
        return (replica, ((my_x + dx) % 4) * 2 + (my_zl + dz) % 2)

    def twin(dy, dzh, dcore):
        return ((((my_y + dy) % 4) * 2 + (my_zh + dzh) % 2) * 2 + (my_core + dcore) % 2, expert)

    core_twin = twin(0, 0, 1)
    z_twin = twin(0, 1, 0)
    y_twins = [twin(dy, 0, 0) for dy in (1, 2, 3)]

    barrier = pltpu.get_barrier_semaphore()
    partners = [peer(*offset) for offset in OFFSETS[:OWN]] + y_twins + [core_twin, z_twin]
    for partner in partners:
        pl.semaphore_signal(barrier, inc=1, device_id=partner, device_id_type=MESH)

    loads = {}
    pairs = dict(
        ids=(ids_hbm, ids), tokens=(tokens_hbm, tokens), logits=(logits_hbm, logits), grads=(grads_hbm, grads),
        other0=(drift_hbm.at[0, :, 1 - my_core], drift_other.at[:, 0]),
        other1=(drift_hbm.at[1, :, 1 - my_core], drift_other.at[:, 1]),
        mine0=(drift_hbm.at[0, :, my_core], drift_mine.at[:, 0]),
        mine1=(drift_hbm.at[1, :, my_core], drift_mine.at[:, 1]),
        gate=(gate_hbm, gate_w), up=(up_hbm, up_w), down=(down_hbm, down_w),
        outer=(outer_hbm, outer), momentum=(momentum_hbm, momentum),
    )
    for number, (name, (source, target)) in enumerate(pairs.items()):
        loads[name] = pltpu.make_async_copy(source, target, local_sem.at[number])
        loads[name].start()

    def remote(source, target, sems, device):
        return pltpu.make_async_remote_copy(
            src_ref=source, dst_ref=target, send_sem=sems[0], recv_sem=sems[1], device_id=device, device_id_type=MESH
        )

    def spread(send, recv, kind, forward):
        copies = []
        for block, (dx, dz) in enumerate(OFFSETS[:OWN]):
            device = peer(dx, dz) if forward else peer(-dx % 4, -dz % 2)
            sems = (send_sem.at[kind, block], recv_sem.at[kind, block])
            copies.append(remote(send.at[block], recv.at[block], sems, device))
        return copies

    token_copies = spread(token_send, token_recv, 0, True)
    weighted_copies = spread(weighted_send, weighted_recv, 1, True)
    back_copies = spread(back_send, back_out, 2, False)
    dots_copies = spread(dots_send, dots_recv, 3, False)

    loads["ids"].wait()
    id_row = ids[...]
    row = lax.broadcasted_iota(jnp.int32, (16, 128), 0)
    named = jnp.full((16, 128), -1, jnp.int32)
    for block, offset in enumerate(OFFSETS):
        named = jnp.where(row == block, peer(*offset)[1], named)
    onehot = jnp.where(named == id_row, 1.0, 0.0)
    before_mask = lax.broadcasted_iota(jnp.int32, (128, 128), 0) < lax.broadcasted_iota(jnp.int32, (128, 128), 1)
    before = dot(onehot.astype(jnp.bfloat16), jnp.where(before_mask, 1.0, 0.0).astype(jnp.bfloat16))
    slot = jnp.sum(onehot * (before + f32(row) * CAP), axis=0, keepdims=True)
    slot_row = lax.broadcasted_iota(jnp.int32, (ROWS, 128), 0)
    select = jnp.where(slot_row == slot.astype(jnp.int32), 1.0, 0.0).astype(jnp.bfloat16)
    select_out[...] = select

    def place(part, values, send, recv):
        first = part * GROUP
        wire = to_wire(dot(select[first * CAP : (first + GROUP) * CAP], values))
        if part == 0:
            send[0:GROUP] = wire
        else:
            send[GROUP:OWN] = wire[: OWN - GROUP]
            recv[OWN] = wire[OWN - GROUP]

    loads["tokens"].wait()
    values = tokens[...]
    place(0, values, token_send, token_recv)
    pl.semaphore_wait(barrier, len(partners))
    for block in (2, 3, 0, 1):
        token_copies[block].start()

    core_sum = remote(core_send, core_recv, (core_sems.at[0], core_sems.at[1]), core_twin)
    loads["other0"].wait()
    loads["other1"].wait()
    core_send[...] = drift_other[...].astype(jnp.bfloat16)
    core_sum.start()

    loads["logits"].wait()
    scores = logits[...]
    powers = jnp.exp(scores - jnp.max(scores, axis=0, keepdims=True))
    probability = powers / jnp.sum(powers, axis=0, keepdims=True)
    column = jnp.transpose(jnp.broadcast_to(probability[0:1, :], (128, 128)))
    loads["grads"].wait()
    weighted = (f32(grads[...]) * jnp.concatenate([column] * (D // 128), axis=1)).astype(jnp.bfloat16)
    place(0, weighted, weighted_send, weighted_recv)
    for block in (2, 3, 0, 1):
        weighted_copies[block].start()
    place(1, values, token_send, token_recv)
    for copy in token_copies[GROUP:]:
        copy.start()
    place(1, weighted, weighted_send, weighted_recv)
    weighted_copies[GROUP].start()
    weighted_copies[GROUP + 1].start()

    loads["mine0"].wait()
    loads["mine1"].wait()
    core_sum.wait()
    y_send[...] = (drift_mine[...] + f32(core_recv[...])).astype(jnp.bfloat16)
    y_sum = []
    for step in range(3):
        there = (my_y + step + 1) % 4
        copy = remote(
            y_send.at[pl.ds(there * 2, 2)], y_recv.at[step], (y_sems.at[0, step], y_sems.at[1, step]), y_twins[step]
        )
        copy.start()
        y_sum.append(copy)

    def front_in(part):
        first = part * GROUP
        rows = pl.ds(first * CAP, GROUP_ROWS)
        count = GROUP if part == 0 else OWN - GROUP
        for copy in token_copies[first : first + count]:
            copy.wait_recv()
        inputs = from_wire(token_recv[first : first + GROUP])
        x_keep[rows, :] = inputs
        if part == 0:
            loads["gate"].wait()
            loads["up"].wait()
        gate = dot(inputs, gate_w[...])
        up = dot(inputs, up_w[...])
        sigmoid = 1.0 / (1.0 + jnp.exp(-gate))
        silu = gate * sigmoid
        active = silu * up
        active_keep[rows, :] = active.astype(jnp.bfloat16)
        return inputs, gate, up, sigmoid, silu, active

    def front_out(part, kept):
        inputs, gate, up, sigmoid, silu, active = kept
        first = part * GROUP
        rows = pl.ds(first * CAP, GROUP_ROWS)
        count = GROUP if part == 0 else OWN - GROUP
        for copy in weighted_copies[first : first + count]:
            copy.wait_recv()
        upstream = from_wire(weighted_recv[first : first + GROUP])
        weighted_keep[rows, :] = upstream
        if part == 0:
            loads["down"].wait()
        grad_active = dot(upstream, down_w[...], 1, 1)
        scalars = jnp.sum(grad_active * active, axis=1, keepdims=True)
        dgate = (grad_active * up * sigmoid * (1.0 + gate * (1.0 - sigmoid))).astype(jnp.bfloat16)
        dup = (grad_active * silu).astype(jnp.bfloat16)
        dgate_keep[rows, :] = dgate
        dup_keep[rows, :] = dup
        lane = lax.broadcasted_iota(jnp.int32, (8, 128), 1)
        for block in range(GROUP):
            eights = [jnp.broadcast_to(scalars[block * CAP + 8 * i : block * CAP + 8 * i + 8], (8, 128)) for i in range(3)]
            packed = jnp.where(lane < 32, eights[0], jnp.where(lane < 64, eights[1], eights[2]))
            if first + block == OWN:
                dots_recv[OWN] = packed
            else:
                dots_send[first + block] = packed
        wire = to_wire(dot(dgate, gate_w[...], 1, 1) + dot(dup, up_w[...], 1, 1))
        if part == 0:
            back_send[0:GROUP] = wire
        else:
            back_send[GROUP:OWN] = wire[: OWN - GROUP]
            back_out[OWN] = wire[OWN - GROUP]

    def gather(part, sems, device):
        return remote(part, part, sems, device)

    z_sum = remote(z_send.at[1 - my_zh], z_recv, (z_sems.at[0], z_sems.at[1]), z_twin)
    near = whole_out.at[my_core, my_y, my_zh]
    far = whole_out.at[my_core, my_y, 1 - my_zh]
    z_gather = gather(near, (z_sems.at[2], z_sems.at[3]), z_twin)
    y_near = [gather(near, (y_sems.at[2, step], y_sems.at[3, step]), y_twins[step]) for step in range(3)]
    y_far = [gather(far, (y_sems.at[4, step], y_sems.at[5, step]), y_twins[step]) for step in range(3)]
    core_near = gather(whole_out.at[my_core, :, my_zh], (core_sems.at[2], core_sems.at[3]), core_twin)
    core_far = gather(whole_out.at[my_core, :, 1 - my_zh], (core_sems.at[4], core_sems.at[5]), core_twin)

    def start(copies):
        for copy in copies:
            copy.start()

    def wait(copies):
        for copy in copies:
            copy.wait()

    kept = front_in(0)
    wait(y_sum)
    mine = pl.ds(my_y * 2, 2)
    y_total[...] = drift_mine[mine] + f32(core_recv[mine]) + f32(y_recv[0]) + f32(y_recv[1]) + f32(y_recv[2])
    z_send[...] = y_total[...].astype(jnp.bfloat16)
    z_sum.start()
    start(weighted_copies[GROUP + 2 :])
    front_out(0, kept)
    start(dots_copies[:GROUP] + back_copies[:2])
    kept = front_in(1)
    loads["outer"].wait()
    loads["momentum"].wait()
    z_sum.wait()
    average = (jnp.where(my_zh == 0, y_total[0], y_total[1]) + f32(z_recv[...])) / REPLICAS
    average_out[...] = average
    moment = momentum_rate * momentum[...] + average
    stepped = outer[...] - outer_rate * (average + momentum_rate * moment)
    near[...] = stepped.astype(jnp.bfloat16)
    start([z_gather] + y_near)
    start(back_copies[2:GROUP])
    front_out(1, kept)
    start(dots_copies[GROUP:] + back_copies[GROUP:])
    z_gather.wait()
    start(y_far)
    wait(y_near)
    core_near.start()

    def wide_tile(index, carry):
        columns = pl.ds(pl.multiple_of(index * 256, 256), 256)
        inputs = x_keep[:, columns]
        grad_gate_out[columns, :] = dot(inputs, dgate_keep[...], 0, 0).astype(jnp.bfloat16)
        grad_up_out[columns, :] = dot(inputs, dup_keep[...], 0, 0).astype(jnp.bfloat16)
        return carry

    def down_tile(index, carry):
        columns = pl.ds(pl.multiple_of(index * 128, 128), 128)
        grad_down_out[columns, :] = dot(active_keep[:, columns], weighted_keep[...], 0, 0).astype(jnp.bfloat16)
        return carry

    lax.fori_loop(0, D // 256, wide_tile, 0)
    wait(y_far)
    core_far.start()
    lax.fori_loop(0, FF // 128, down_tile, 0)

    for copy in token_copies + weighted_copies:
        copy.wait_send()
    wait(dots_copies)
    for block in range(BLOCKS):
        for i in range(3):
            first = block * CAP + 8 * i
            dots_out[first : first + 8, :] = jnp.broadcast_to(dots_recv[block][:, 32 * i : 32 * i + 1], (8, 128))
    wait(back_copies)
    wait([core_near, core_far])


def exchange(ids, logits, tokens, grads, w_gate, w_up, w_down, drift, outer, momentum):
    bf16, wide = jnp.bfloat16, jnp.float32
    anywhere = pl.BlockSpec(memory_space=pltpu.HBM)
    inside = pl.BlockSpec(memory_space=pltpu.VMEM)
    outs = [
        ((D, FF), bf16), ((D, FF), bf16), ((FF, D), bf16),
        ((BLOCKS, 2 * CAP, HALF), bf16), ((ROWS, 128), bf16), ((ROWS, 128), wide),
        ((2, 128, 128), wide), ((2, 4, 2, 2, 128, 128), bf16),
    ]
    wire = pltpu.VMEM((BLOCKS, 2 * CAP, HALF), bf16)
    dots = pltpu.VMEM((BLOCKS, 8, 128), wide)
    dma = pltpu.SemaphoreType.DMA
    return pl.pallas_call(
        exchange_kernel,
        out_shape=[jax.ShapeDtypeStruct(*out) for out in outs],
        in_specs=[anywhere] * 10,
        out_specs=[inside] * len(outs),
        scratch_shapes=[
            pltpu.VMEM((ROWS, D), bf16), pltpu.VMEM((ROWS, D), bf16), pltpu.VMEM((ROWS, FF), bf16),
            pltpu.VMEM((ROWS, FF), bf16), pltpu.VMEM((ROWS, FF), bf16), pltpu.VMEM((2, 2, 128, 128), wide),
            pltpu.VMEM((1, 128), jnp.int32), pltpu.VMEM((8, 128), wide),
            pltpu.VMEM((128, D), bf16), pltpu.VMEM((128, D), bf16),
            pltpu.VMEM((D, FF), bf16), pltpu.VMEM((D, FF), bf16), pltpu.VMEM((FF, D), bf16),
            pltpu.VMEM((8, 2, 128, 128), wide), pltpu.VMEM((8, 2, 128, 128), wide),
            pltpu.VMEM((2, 128, 128), wide), pltpu.VMEM((2, 128, 128), wide),
            wire, wire, wire, wire, wire, dots, dots,
            pltpu.VMEM((8, 2, 128, 128), bf16), pltpu.VMEM((8, 2, 128, 128), bf16),
            pltpu.VMEM((8, 2, 128, 128), bf16), pltpu.VMEM((3, 2, 2, 128, 128), bf16),
            pltpu.VMEM((2, 2, 128, 128), bf16), pltpu.VMEM((2, 128, 128), bf16),
            dma((13,)), dma((4, OWN)), dma((4, OWN)), dma((6,)), dma((6, 3)), dma((4,)),
        ],
        compiler_params=pltpu.CompilerParams(
            collective_id=0, has_side_effects=True, vmem_limit_bytes=32 << 20
        ),
        cost_estimate=pl.CostEstimate(flops=5 * 2 * ROWS * D * FF, bytes_accessed=16 << 20, transcendentals=ROWS * FF),
    )(*[pltpu.with_memory_space_constraint(a, pltpu.HBM) for a in (ids, logits, tokens, grads, w_gate, w_up, w_down, drift, outer, momentum)])


def finish_kernel(
    gate_in, up_in, down_in, back, select, dots, average, whole, logits, outer, momentum, inner,
    grad_tokens, grad_logits, grad_gate, grad_up, grad_down, new_outer, new_momentum, merged,
    tokens_keep, logits_keep, outer_keep, momentum_keep, merged_keep, sems,
):
    copies = []

    def put(source, target):
        copies.append(pltpu.make_async_copy(source, target, sems.at[len(copies)]))
        copies[-1].start()

    for source, target in ((gate_in, grad_gate), (up_in, grad_up), (down_in, grad_down)):
        size = source.shape[0] // 4
        for part in range(4):
            put(source.at[pl.ds(part * size, size)], target.at[pl.ds(part * size, size)])
    grad_tokens_rows = dot(select[...], from_wire(back[...]), 0, 0).astype(jnp.bfloat16)
    tokens_keep[...] = grad_tokens_rows
    put(tokens_keep, grad_tokens)
    moment = momentum_rate * momentum[...] + average[...]
    momentum_keep[...] = moment
    put(momentum_keep, new_momentum)
    outer_keep[...] = outer[...] - outer_rate * (average[...] + momentum_rate * moment)
    put(outer_keep, new_outer)
    scores = logits[...]
    powers = jnp.exp(scores - jnp.max(scores, axis=0, keepdims=True))
    probability = powers / jnp.sum(powers, axis=0, keepdims=True)
    scalar = jnp.sum(f32(select[...]) * dots[...], axis=0, keepdims=True)
    first = lax.broadcasted_iota(jnp.int32, (8, 128), 0) == 0
    logits_keep[...] = jnp.where(first, scalar * (1.0 - probability), -probability * scalar)
    put(logits_keep, grad_logits)
    for y in range(4):
        for zh in range(2):
            for core in range(2):
                rows = pl.ds(((y * 2 + zh) * 2 + core) * 128, 128)
                for layer in range(2):
                    merged_keep[layer, rows, :] = (
                        mix_rate * f32(inner[layer, rows, :]) + (1.0 - mix_rate) * f32(whole[core, y, zh, layer])
                    ).astype(jnp.bfloat16)
    put(merged_keep, merged)
    for copy in copies:
        copy.wait()


def finish(gate_in, up_in, down_in, back, select, dots, average, whole, logits, outer, momentum, inner):
    bf16, wide = jnp.bfloat16, jnp.float32
    anywhere = pl.BlockSpec(memory_space=pl.ANY)
    inside = pl.BlockSpec(memory_space=pltpu.VMEM)
    return pl.pallas_call(
        finish_kernel,
        out_shape=[
            jax.ShapeDtypeStruct((128, D), bf16), jax.ShapeDtypeStruct((8, 128), wide),
            jax.ShapeDtypeStruct((D, FF), bf16), jax.ShapeDtypeStruct((D, FF), bf16),
            jax.ShapeDtypeStruct((FF, D), bf16), jax.ShapeDtypeStruct((2, 128, 128), wide),
            jax.ShapeDtypeStruct((2, 128, 128), wide), jax.ShapeDtypeStruct((2, D, 128), bf16),
        ],
        in_specs=[anywhere] * 3 + [inside] * 9,
        out_specs=[anywhere] * 8,
        scratch_shapes=[
            pltpu.VMEM((128, D), bf16), pltpu.VMEM((8, 128), wide), pltpu.VMEM((2, 128, 128), wide),
            pltpu.VMEM((2, 128, 128), wide), pltpu.VMEM((2, D, 128), bf16), pltpu.SemaphoreType.DMA((17,)),
        ],
        compiler_params=pltpu.CompilerParams(vmem_limit_bytes=20 << 20),
        cost_estimate=pl.CostEstimate(flops=2 * ROWS * D * 128, bytes_accessed=22 << 20, transcendentals=1024),
    )(gate_in, up_in, down_in, back, select, dots, average, whole, logits, outer, momentum, inner)


def body(tokens, route_ids, route_logits, grad_out, w_gate, w_up, w_down, drift, outer, momentum, inner_now):
    logits = route_logits.T
    sent = exchange(
        route_ids.reshape(1, 128), logits, tokens, grad_out, w_gate[0, 0], w_up[0, 0], w_down[0, 0],
        drift.reshape(2, 8, 2, 128, 128), outer, momentum,
    )
    grad_tokens, grad_logits, grad_gate, grad_up, grad_down, new_outer, new_momentum, merged = finish(
        *sent, logits, outer, momentum, inner_now[0]
    )
    return (
        grad_tokens, grad_logits.T, grad_gate[None, None], grad_up[None, None], grad_down[None, None],
        new_outer, new_momentum, merged[None],
    )


def solution(mesh):
    both = P(("replica", "expert"), None)
    pair = P("replica", "expert", None, None)
    part = P("replica", None, None, "expert")
    shard = P(None, "replica", "expert")
    in_specs = (both, both, both, both, pair, pair, pair, part, shard, shard, part)
    out_specs = (both, both, pair, pair, pair, shard, shard, part)
    return jax.shard_map(body, mesh=mesh, in_specs=in_specs, out_specs=out_specs, check_vma=False)
```

```python
import jax
import jax.numpy as jnp
from jax import lax
from jax.experimental import pallas as pl
from jax.experimental.pallas import tpu as pltpu
from jax.sharding import PartitionSpec as P

MESH = pl.DeviceIdType.MESH
D = 2048
FF = 768
HALF = D // 2
CAP = 24
BLOCKS = 8
ROWS = BLOCKS * CAP
GROUP = 4
GROUP_ROWS = GROUP * CAP
REPLICAS = 16

momentum_rate = 0.9
outer_rate = 0.7
mix_rate = 0.5

OFFSETS = ((1, 0), (3, 0), (1, 1), (3, 1), (2, 1), (2, 0), (0, 1), (0, 0))
OWN = 7


def f32(value):
    return value.astype(jnp.float32)


def to_wire(rows):
    blocks = rows.reshape(-1, CAP, D)
    return jnp.concatenate([blocks[:, :, :HALF], blocks[:, :, HALF:]], axis=1).astype(jnp.bfloat16)


def from_wire(blocks):
    wide = f32(blocks)
    count = wide.shape[0]
    left = wide[:, :CAP, :].reshape(count * CAP, HALF)
    right = wide[:, CAP:, :].reshape(count * CAP, HALF)
    return jnp.concatenate([left, right], axis=1).astype(jnp.bfloat16)


def dot(left, right, left_axis=1, right_axis=0):
    return lax.dot_general(
        left, right, (((left_axis,), (right_axis,)), ((), ())), preferred_element_type=jnp.float32
    )


def exchange_kernel(
    ids_hbm, logits_hbm, tokens_hbm, grads_hbm, gate_hbm, up_hbm, down_hbm, drift_hbm, outer_hbm, momentum_hbm,
    grad_gate_out, grad_up_out, grad_down_out, back_out, select_out, dots_out, average_out, whole_out,
    x_keep, weighted_keep, active_keep, dgate_keep, dup_keep, y_total, ids, logits, tokens, grads, gate_w, up_w, down_w, drift_mine, drift_other, outer, momentum,
    token_send, token_recv, weighted_send, weighted_recv, back_send, dots_send, dots_recv,
    core_send, core_recv, y_send, y_recv, z_send, z_recv,
    local_sem, send_sem, recv_sem, core_sems, y_sems, z_sems,
):
    replica = lax.axis_index("replica")
    expert = lax.axis_index("expert")
    my_y, my_zh, my_core = replica // 4, (replica // 2) % 2, replica % 2
    my_x, my_zl = expert // 2, expert % 2

    def peer(dx, dz):
        return (replica, ((my_x + dx) % 4) * 2 + (my_zl + dz) % 2)

    def twin(dy, dzh, dcore):
        return ((((my_y + dy) % 4) * 2 + (my_zh + dzh) % 2) * 2 + (my_core + dcore) % 2, expert)

    core_twin = twin(0, 0, 1)
    z_twin = twin(0, 1, 0)
    y_twins = [twin(dy, 0, 0) for dy in (1, 2, 3)]

    barrier = pltpu.get_barrier_semaphore()
    partners = [peer(*offset) for offset in OFFSETS[:OWN]] + y_twins + [core_twin, z_twin]
    for partner in partners:
        pl.semaphore_signal(barrier, inc=1, device_id=partner, device_id_type=MESH)

    loads = {}
    pairs = dict(
        ids=(ids_hbm, ids), tokens=(tokens_hbm, tokens), logits=(logits_hbm, logits), grads=(grads_hbm, grads),
        other0=(drift_hbm.at[0, :, 1 - my_core], drift_other.at[:, 0]),
        other1=(drift_hbm.at[1, :, 1 - my_core], drift_other.at[:, 1]),
        mine0=(drift_hbm.at[0, :, my_core], drift_mine.at[:, 0]),
        mine1=(drift_hbm.at[1, :, my_core], drift_mine.at[:, 1]),
        gate=(gate_hbm, gate_w), up=(up_hbm, up_w), down=(down_hbm, down_w),
        outer=(outer_hbm, outer), momentum=(momentum_hbm, momentum),
    )
    for number, (name, (source, target)) in enumerate(pairs.items()):
        loads[name] = pltpu.make_async_copy(source, target, local_sem.at[number])
        loads[name].start()

    def remote(source, target, sems, device):
        return pltpu.make_async_remote_copy(
            src_ref=source, dst_ref=target, send_sem=sems[0], recv_sem=sems[1], device_id=device, device_id_type=MESH
        )

    def spread(send, recv, kind, forward):
        copies = []
        for block, (dx, dz) in enumerate(OFFSETS[:OWN]):
            device = peer(dx, dz) if forward else peer(-dx % 4, -dz % 2)
            sems = (send_sem.at[kind, block], recv_sem.at[kind, block])
            copies.append(remote(send.at[block], recv.at[block], sems, device))
        return copies

    token_copies = spread(token_send, token_recv, 0, True)
    weighted_copies = spread(weighted_send, weighted_recv, 1, True)
    back_copies = spread(back_send, back_out, 2, False)
    dots_copies = spread(dots_send, dots_recv, 3, False)

    loads["ids"].wait()
    id_row = ids[...]
    row = lax.broadcasted_iota(jnp.int32, (16, 128), 0)
    named = jnp.full((16, 128), -1, jnp.int32)
    for block, offset in enumerate(OFFSETS):
        named = jnp.where(row == block, peer(*offset)[1], named)
    onehot = jnp.where(named == id_row, 1.0, 0.0)
    before_mask = lax.broadcasted_iota(jnp.int32, (128, 128), 0) < lax.broadcasted_iota(jnp.int32, (128, 128), 1)
    before = dot(onehot.astype(jnp.bfloat16), jnp.where(before_mask, 1.0, 0.0).astype(jnp.bfloat16))
    slot = jnp.sum(onehot * (before + f32(row) * CAP), axis=0, keepdims=True)
    slot_row = lax.broadcasted_iota(jnp.int32, (ROWS, 128), 0)
    select = jnp.where(slot_row == slot.astype(jnp.int32), 1.0, 0.0).astype(jnp.bfloat16)
    select_out[...] = select

    def place(part, values, send, recv):
        first = part * GROUP
        wire = to_wire(dot(select[first * CAP : (first + GROUP) * CAP], values))
        if part == 0:
            send[0:GROUP] = wire
        else:
            send[GROUP:OWN] = wire[: OWN - GROUP]
            recv[OWN] = wire[OWN - GROUP]

    loads["tokens"].wait()
    values = tokens[...]
    place(0, values, token_send, token_recv)
    pl.semaphore_wait(barrier, len(partners))
    for block in (2, 3, 0, 1):
        token_copies[block].start()

    core_sum = remote(core_send, core_recv, (core_sems.at[0], core_sems.at[1]), core_twin)
    loads["other0"].wait()
    loads["other1"].wait()
    core_send[...] = drift_other[...].astype(jnp.bfloat16)
    core_sum.start()

    loads["logits"].wait()
    scores = logits[...]
    powers = jnp.exp(scores - jnp.max(scores, axis=0, keepdims=True))
    probability = powers / jnp.sum(powers, axis=0, keepdims=True)
    column = jnp.transpose(jnp.broadcast_to(probability[0:1, :], (128, 128)))
    loads["grads"].wait()
    weighted = (f32(grads[...]) * jnp.concatenate([column] * (D // 128), axis=1)).astype(jnp.bfloat16)
    place(0, weighted, weighted_send, weighted_recv)
    for block in (2, 3, 0, 1):
        weighted_copies[block].start()
    place(1, values, token_send, token_recv)
    for copy in token_copies[GROUP:]:
        copy.start()
    place(1, weighted, weighted_send, weighted_recv)
    weighted_copies[GROUP].start()
    weighted_copies[GROUP + 1].start()

    loads["mine0"].wait()
    loads["mine1"].wait()
    core_sum.wait()
    y_send[...] = (drift_mine[...] + f32(core_recv[...])).astype(jnp.bfloat16)
    y_sum = []
    for step in (1, 0, 2):
        there = (my_y + step + 1) % 4
        copy = remote(
            y_send.at[pl.ds(there * 2, 2)], y_recv.at[step], (y_sems.at[0, step], y_sems.at[1, step]), y_twins[step]
        )
        copy.start()
        y_sum.append(copy)

    def front_in(part):
        first = part * GROUP
        rows = pl.ds(first * CAP, GROUP_ROWS)
        count = GROUP if part == 0 else OWN - GROUP
        for copy in token_copies[first : first + count]:
            copy.wait_recv()
        inputs = from_wire(token_recv[first : first + GROUP])
        x_keep[rows, :] = inputs
        if part == 0:
            loads["gate"].wait()
            loads["up"].wait()
        gate = dot(inputs, gate_w[...])
        up = dot(inputs, up_w[...])
        sigmoid = 1.0 / (1.0 + jnp.exp(-gate))
        silu = gate * sigmoid
        active = silu * up
        active_keep[rows, :] = active.astype(jnp.bfloat16)
        return inputs, gate, up, sigmoid, silu, active

    def front_out(part, kept):
        inputs, gate, up, sigmoid, silu, active = kept
        first = part * GROUP
        rows = pl.ds(first * CAP, GROUP_ROWS)
        count = GROUP if part == 0 else OWN - GROUP
        for copy in weighted_copies[first : first + count]:
            copy.wait_recv()
        upstream = from_wire(weighted_recv[first : first + GROUP])
        weighted_keep[rows, :] = upstream
        if part == 0:
            loads["down"].wait()
        grad_active = dot(upstream, down_w[...], 1, 1)
        scalars = jnp.sum(grad_active * active, axis=1, keepdims=True)
        dgate = (grad_active * up * sigmoid * (1.0 + gate * (1.0 - sigmoid))).astype(jnp.bfloat16)
        dup = (grad_active * silu).astype(jnp.bfloat16)
        dgate_keep[rows, :] = dgate
        dup_keep[rows, :] = dup
        lane = lax.broadcasted_iota(jnp.int32, (8, 128), 1)
        for block in range(GROUP):
            eights = [jnp.broadcast_to(scalars[block * CAP + 8 * i : block * CAP + 8 * i + 8], (8, 128)) for i in range(3)]
            packed = jnp.where(lane < 32, eights[0], jnp.where(lane < 64, eights[1], eights[2]))
            if first + block == OWN:
                dots_recv[OWN] = packed
            else:
                dots_send[first + block] = packed
        wire = to_wire(dot(dgate, gate_w[...], 1, 1) + dot(dup, up_w[...], 1, 1))
        if part == 0:
            back_send[0:GROUP] = wire
        else:
            back_send[GROUP:OWN] = wire[: OWN - GROUP]
            back_out[OWN] = wire[OWN - GROUP]

    def gather(part, sems, device):
        return remote(part, part, sems, device)

    z_sum = remote(z_send.at[1 - my_zh], z_recv, (z_sems.at[0], z_sems.at[1]), z_twin)
    near = whole_out.at[my_core, my_y, my_zh]
    far = whole_out.at[my_core, my_y, 1 - my_zh]
    z_gather = gather(near, (z_sems.at[2], z_sems.at[3]), z_twin)
    y_near = [gather(near, (y_sems.at[2, step], y_sems.at[3, step]), y_twins[step]) for step in (1, 0, 2)]
    y_far = [gather(far, (y_sems.at[4, step], y_sems.at[5, step]), y_twins[step]) for step in (1, 0, 2)]
    core_near = gather(whole_out.at[my_core, :, my_zh], (core_sems.at[2], core_sems.at[3]), core_twin)
    core_far = gather(whole_out.at[my_core, :, 1 - my_zh], (core_sems.at[4], core_sems.at[5]), core_twin)

    def start(copies):
        for copy in copies:
            copy.start()

    def wait(copies):
        for copy in copies:
            copy.wait()

    kept = front_in(0)
    wait(y_sum)
    mine = pl.ds(my_y * 2, 2)
    y_total[...] = drift_mine[mine] + f32(core_recv[mine]) + f32(y_recv[0]) + f32(y_recv[1]) + f32(y_recv[2])
    z_send[...] = y_total[...].astype(jnp.bfloat16)
    z_sum.start()
    start(weighted_copies[GROUP + 2 :])
    front_out(0, kept)
    start(dots_copies[:GROUP] + back_copies[:2])
    kept = front_in(1)
    loads["outer"].wait()
    loads["momentum"].wait()
    z_sum.wait()
    average = (jnp.where(my_zh == 0, y_total[0], y_total[1]) + f32(z_recv[...])) / REPLICAS
    average_out[...] = average
    moment = momentum_rate * momentum[...] + average
    stepped = outer[...] - outer_rate * (average + momentum_rate * moment)
    near[...] = stepped.astype(jnp.bfloat16)
    start([z_gather] + y_near)
    start(back_copies[2:GROUP])
    front_out(1, kept)
    start(dots_copies[GROUP:] + back_copies[GROUP:])
    z_gather.wait()
    start(y_far)
    wait(y_near)
    core_near.start()

    def wide_tile(index, carry):
        columns = pl.ds(pl.multiple_of(index * 256, 256), 256)
        inputs = x_keep[:, columns]
        grad_gate_out[columns, :] = dot(inputs, dgate_keep[...], 0, 0).astype(jnp.bfloat16)
        grad_up_out[columns, :] = dot(inputs, dup_keep[...], 0, 0).astype(jnp.bfloat16)
        return carry

    def down_tile(index, carry):
        columns = pl.ds(pl.multiple_of(index * 128, 128), 128)
        grad_down_out[columns, :] = dot(active_keep[:, columns], weighted_keep[...], 0, 0).astype(jnp.bfloat16)
        return carry

    lax.fori_loop(0, D // 256, wide_tile, 0)
    wait(y_far)
    core_far.start()
    lax.fori_loop(0, FF // 128, down_tile, 0)

    for copy in token_copies + weighted_copies:
        copy.wait_send()
    wait(dots_copies)
    for block in range(BLOCKS):
        for i in range(3):
            first = block * CAP + 8 * i
            dots_out[first : first + 8, :] = jnp.broadcast_to(dots_recv[block][:, 32 * i : 32 * i + 1], (8, 128))
    wait(back_copies)
    wait([core_near, core_far])


def exchange(ids, logits, tokens, grads, w_gate, w_up, w_down, drift, outer, momentum):
    bf16, wide = jnp.bfloat16, jnp.float32
    anywhere = pl.BlockSpec(memory_space=pltpu.HBM)
    inside = pl.BlockSpec(memory_space=pltpu.VMEM)
    outs = [
        ((D, FF), bf16), ((D, FF), bf16), ((FF, D), bf16),
        ((BLOCKS, 2 * CAP, HALF), bf16), ((ROWS, 128), bf16), ((ROWS, 128), wide),
        ((2, 128, 128), wide), ((2, 4, 2, 2, 128, 128), bf16),
    ]
    wire = pltpu.VMEM((BLOCKS, 2 * CAP, HALF), bf16)
    dots = pltpu.VMEM((BLOCKS, 8, 128), wide)
    dma = pltpu.SemaphoreType.DMA
    return pl.pallas_call(
        exchange_kernel,
        out_shape=[jax.ShapeDtypeStruct(*out) for out in outs],
        in_specs=[anywhere] * 10,
        out_specs=[inside] * len(outs),
        scratch_shapes=[
            pltpu.VMEM((ROWS, D), bf16), pltpu.VMEM((ROWS, D), bf16), pltpu.VMEM((ROWS, FF), bf16),
            pltpu.VMEM((ROWS, FF), bf16), pltpu.VMEM((ROWS, FF), bf16), pltpu.VMEM((2, 2, 128, 128), wide),
            pltpu.VMEM((1, 128), jnp.int32), pltpu.VMEM((8, 128), wide),
            pltpu.VMEM((128, D), bf16), pltpu.VMEM((128, D), bf16),
            pltpu.VMEM((D, FF), bf16), pltpu.VMEM((D, FF), bf16), pltpu.VMEM((FF, D), bf16),
            pltpu.VMEM((8, 2, 128, 128), wide), pltpu.VMEM((8, 2, 128, 128), wide),
            pltpu.VMEM((2, 128, 128), wide), pltpu.VMEM((2, 128, 128), wide),
            wire, wire, wire, wire, wire, dots, dots,
            pltpu.VMEM((8, 2, 128, 128), bf16), pltpu.VMEM((8, 2, 128, 128), bf16),
            pltpu.VMEM((8, 2, 128, 128), bf16), pltpu.VMEM((3, 2, 2, 128, 128), bf16),
            pltpu.VMEM((2, 2, 128, 128), bf16), pltpu.VMEM((2, 128, 128), bf16),
            dma((13,)), dma((4, OWN)), dma((4, OWN)), dma((6,)), dma((6, 3)), dma((4,)),
        ],
        compiler_params=pltpu.CompilerParams(
            collective_id=0, has_side_effects=True, vmem_limit_bytes=32 << 20
        ),
        cost_estimate=pl.CostEstimate(flops=5 * 2 * ROWS * D * FF, bytes_accessed=16 << 20, transcendentals=ROWS * FF),
    )(*[pltpu.with_memory_space_constraint(a, pltpu.HBM) for a in (ids, logits, tokens, grads, w_gate, w_up, w_down, drift, outer, momentum)])


def finish_kernel(
    gate_in, up_in, down_in, back, select, dots, average, whole, logits, outer, momentum, inner,
    grad_tokens, grad_logits, grad_gate, grad_up, grad_down, new_outer, new_momentum, merged,
    tokens_keep, logits_keep, outer_keep, momentum_keep, merged_keep, sems,
):
    copies = []

    def put(source, target):
        copies.append(pltpu.make_async_copy(source, target, sems.at[len(copies)]))
        copies[-1].start()

    for source, target in ((gate_in, grad_gate), (up_in, grad_up), (down_in, grad_down)):
        size = source.shape[0] // 4
        for part in range(4):
            put(source.at[pl.ds(part * size, size)], target.at[pl.ds(part * size, size)])
    grad_tokens_rows = dot(select[...], from_wire(back[...]), 0, 0).astype(jnp.bfloat16)
    tokens_keep[...] = grad_tokens_rows
    put(tokens_keep, grad_tokens)
    moment = momentum_rate * momentum[...] + average[...]
    momentum_keep[...] = moment
    put(momentum_keep, new_momentum)
    outer_keep[...] = outer[...] - outer_rate * (average[...] + momentum_rate * moment)
    put(outer_keep, new_outer)
    scores = logits[...]
    powers = jnp.exp(scores - jnp.max(scores, axis=0, keepdims=True))
    probability = powers / jnp.sum(powers, axis=0, keepdims=True)
    scalar = jnp.sum(f32(select[...]) * dots[...], axis=0, keepdims=True)
    first = lax.broadcasted_iota(jnp.int32, (8, 128), 0) == 0
    logits_keep[...] = jnp.where(first, scalar * (1.0 - probability), -probability * scalar)
    put(logits_keep, grad_logits)
    for y in range(4):
        for zh in range(2):
            for core in range(2):
                rows = pl.ds(((y * 2 + zh) * 2 + core) * 128, 128)
                for layer in range(2):
                    merged_keep[layer, rows, :] = (
                        mix_rate * f32(inner[layer, rows, :]) + (1.0 - mix_rate) * f32(whole[core, y, zh, layer])
                    ).astype(jnp.bfloat16)
    put(merged_keep, merged)
    for copy in copies:
        copy.wait()


def finish(gate_in, up_in, down_in, back, select, dots, average, whole, logits, outer, momentum, inner):
    bf16, wide = jnp.bfloat16, jnp.float32
    anywhere = pl.BlockSpec(memory_space=pl.ANY)
    inside = pl.BlockSpec(memory_space=pltpu.VMEM)
    return pl.pallas_call(
        finish_kernel,
        out_shape=[
            jax.ShapeDtypeStruct((128, D), bf16), jax.ShapeDtypeStruct((8, 128), wide),
            jax.ShapeDtypeStruct((D, FF), bf16), jax.ShapeDtypeStruct((D, FF), bf16),
            jax.ShapeDtypeStruct((FF, D), bf16), jax.ShapeDtypeStruct((2, 128, 128), wide),
            jax.ShapeDtypeStruct((2, 128, 128), wide), jax.ShapeDtypeStruct((2, D, 128), bf16),
        ],
        in_specs=[anywhere] * 3 + [inside] * 9,
        out_specs=[anywhere] * 8,
        scratch_shapes=[
            pltpu.VMEM((128, D), bf16), pltpu.VMEM((8, 128), wide), pltpu.VMEM((2, 128, 128), wide),
            pltpu.VMEM((2, 128, 128), wide), pltpu.VMEM((2, D, 128), bf16), pltpu.SemaphoreType.DMA((17,)),
        ],
        compiler_params=pltpu.CompilerParams(vmem_limit_bytes=20 << 20),
        cost_estimate=pl.CostEstimate(flops=2 * ROWS * D * 128, bytes_accessed=22 << 20, transcendentals=1024),
    )(gate_in, up_in, down_in, back, select, dots, average, whole, logits, outer, momentum, inner)


def body(tokens, route_ids, route_logits, grad_out, w_gate, w_up, w_down, drift, outer, momentum, inner_now):
    logits = route_logits.T
    sent = exchange(
        route_ids.reshape(1, 128), logits, tokens, grad_out, w_gate[0, 0], w_up[0, 0], w_down[0, 0],
        drift.reshape(2, 8, 2, 128, 128), outer, momentum,
    )
    grad_tokens, grad_logits, grad_gate, grad_up, grad_down, new_outer, new_momentum, merged = finish(
        *sent, logits, outer, momentum, inner_now[0]
    )
    return (
        grad_tokens, grad_logits.T, grad_gate[None, None], grad_up[None, None], grad_down[None, None],
        new_outer, new_momentum, merged[None],
    )


def solution(mesh):
    both = P(("replica", "expert"), None)
    pair = P("replica", "expert", None, None)
    part = P("replica", None, None, "expert")
    shard = P(None, "replica", "expert")
    in_specs = (both, both, both, both, pair, pair, pair, part, shard, shard, part)
    out_specs = (both, both, pair, pair, pair, shard, shard, part)
    return jax.shard_map(body, mesh=mesh, in_specs=in_specs, out_specs=out_specs, check_vma=False)
```
